128 devices in a mesh: author: 8 (over x, core), word: 16 (over y, z).
Axes of the slice: x: 4, y: 4, z: 4, core: 2. Of those that a mesh axis runs over, the one named last changes fastest.
Arguments:
- block_values: bfloat16 [8, 16, 128, 128, 128], P('author', 'word'), as said below
- block_rows: int32 [8, 16, 128], P('author', 'word'), may hold values from 0 to 31, as said below
- block_cols: int32 [8, 16, 128], P('author', 'word'), may hold values from 0 to 127
- block_count: int32 [8, 16], P('author', 'word'), may hold values from 32 to 128, as said below
- omega: bfloat16 [262144, 256], P('word'), may hold values from -6 to 6
Outputs:
- author_basis: bfloat16 [32768, 256], P(('author', 'word'))
- word_basis: bfloat16 [262144, 256], P(('word', 'author'))
The draws below stay inside these ranges and needn't reach their ends.
Inputs may be any that keep to these rules, and one draw needn't show every extreme that they name: `block_values`: entries of slots at or past a device's count are finite and unused. `block_rows`: the 128 slots of one device name distinct (row block, column block) pairs. `block_count`: some device holds exactly 128 live blocks and some other device exactly a quarter of 128.
All inputs are finite; a program needn't handle non-finite values.
Results may differ from the reference program's by a relative error of at most 0.029.
Values may be sent and summed in bfloat16 or wider, within the bound.
No kernel may reach another device: no remote copies, remote signals or barrier semaphores. Data moves between devices by JAX's collectives and lax.ppermute only.
A program may use at most 192 MiB of HBM per device.

```python
import math
import jax
import jax.numpy as jnp
from jax import lax

BS = 128
PANEL = 256
CAP = 128
ITERS = 2
AB = 32
WB = 128
WORDS = 262144
N_AUTHOR = 8
N_WORD = 16


def block_positions(key):
    keys = jax.random.split(key, N_AUTHOR * N_WORD)
    picked = jax.vmap(lambda single: jax.random.permutation(single, AB * WB)[:CAP])(keys)
    return picked.reshape(N_AUTHOR, N_WORD, CAP).astype(jnp.int32)


def draw_block_rows(key, part):
    placed = block_positions(key)
    return (placed // WB).astype(jnp.int32)


def draw_block_cols(key, part):
    placed = block_positions(key)
    return (placed % WB).astype(jnp.int32)


def draw_block_count(key, part):
    key = jax.random.fold_in(key, 5)
    first, second, third, fourth = jax.random.split(key, 4)
    total = N_AUTHOR * N_WORD
    lowest = CAP // 4
    left = jax.random.randint(first, (total,), 0, CAP + 1)
    right = jax.random.randint(second, (total,), 0, CAP + 1)
    counts = jnp.minimum(lowest + left * right // CAP * (CAP - lowest) // CAP, CAP)
    chosen = jax.random.randint(third, (), 0, total)
    other = (chosen + 1 + jax.random.randint(fourth, (), 0, total - 1)) % total
    places = jnp.arange(total, dtype=jnp.int32)
    counts = jnp.where(places == chosen, CAP, counts)
    counts = jnp.where(places == other, lowest, counts)
    return counts.reshape(N_AUTHOR, N_WORD).astype(jnp.int32)


def draw_block_values(key, part):
    key = jax.random.fold_in(key, 3)
    first, second, third = jax.random.split(key, 3)
    shape = (N_AUTHOR, N_WORD, CAP, BS, BS)
    base = jax.random.normal(first, shape, jnp.float32)
    top = math.log(10.0)
    row_scale = jnp.exp(jax.random.uniform(second, (N_AUTHOR, N_WORD, CAP, BS, 1), jnp.float32, 0.0, top))
    col_scale = jnp.exp(jax.random.uniform(third, (N_AUTHOR, N_WORD, CAP, 1, BS), jnp.float32, 0.0, top))
    return (base * row_scale * col_scale * 0.05).astype(jnp.bfloat16)


def block_levels(key, dims, cuts, low, high):
    def one(axis_at, parts):
        heights = jax.random.uniform(jax.random.fold_in(jax.random.fold_in(key, 6), axis_at), (parts,), jnp.float32, low / len(cuts), high / len(cuts))
        return jnp.repeat(jnp.exp(heights), dims[axis_at] // parts).reshape((-1,) + (1,) * (len(dims) - axis_at - 1))

    level = one(*cuts[0])
    for cut in cuts[1:]:
        level = level * one(*cut)
    return level


def scatter_about(stream_key, dims, width, limit, pieces=(), kind=jnp.bfloat16):
    level = block_levels(stream_key, dims, pieces, -0.22, 0.18) if pieces else 1.0
    array = jax.random.normal(stream_key, dims, jnp.float32) * width * level
    return jnp.minimum(jnp.maximum(array, -limit), limit).astype(kind)


def setup_inputs(seed: int = 0) -> dict:
    splits = jax.random.split(jax.random.key(seed), 6)
    return {
        "block_values": draw_block_values(jax.random.fold_in(splits[5], 71), 0),
        "block_rows": draw_block_rows(jax.random.fold_in(splits[5], 71), 0),
        "block_cols": draw_block_cols(jax.random.fold_in(splits[5], 71), 0),
        "block_count": draw_block_count(jax.random.fold_in(splits[5], 71), 0),
        "omega": scatter_about(splits[4], (WORDS, PANEL), 1.0, 6.0, ((0, 16),)),
    }


def local_product(values, rows, cols, count, panel, out_blocks, transpose):
    cap = values.shape[0]
    size = values.shape[1]
    blocks = panel.reshape(-1, size, panel.shape[1])
    live = (jnp.arange(cap, dtype=jnp.int32) < count).astype(jnp.float32)
    if transpose:
        source = blocks[rows]
        target = cols
        prod = jnp.einsum('kji,kjn->kin', values.astype(jnp.float32), source.astype(jnp.float32))
    else:
        source = blocks[cols]
        target = rows
        prod = jnp.einsum('kij,kjn->kin', values.astype(jnp.float32), source.astype(jnp.float32))
    prod = prod * live[:, None, None]
    summed = jax.ops.segment_sum(prod, target, num_segments=out_blocks)
    return summed.reshape(out_blocks * size, -1)

def rounded(term):
    return lax.optimization_barrier(term.astype(jnp.bfloat16)).astype(jnp.float32)

def orthonormal(field, total):
    gram = lax.dot_general(field.astype(jnp.float32), field.astype(jnp.float32), (((0,), (0,)), ((), ())), precision=lax.Precision.HIGHEST, preferred_element_type=jnp.float32) / total
    lower = jnp.linalg.cholesky(gram)
    inverse = jax.scipy.linalg.solve_triangular(lower, jnp.eye(gram.shape[0], dtype=jnp.float32), lower=True)
    return jnp.dot(field.astype(jnp.float32), inverse.T.astype(jnp.float32), precision=lax.Precision.HIGHEST, preferred_element_type=jnp.float32).astype(jnp.bfloat16)

def reference(block_values, block_rows, block_cols, block_count, omega):
    authors = AB * BS * N_AUTHOR
    words = WB * BS * N_WORD
    devices_all = N_AUTHOR * N_WORD
    panel = omega
    author_basis = jnp.zeros((authors, PANEL), jnp.bfloat16)
    for turn in range(ITERS):

        def author_step(index, total):
            arow = index // N_WORD
            wcol = index % N_WORD
            wide = lax.dynamic_slice_in_dim(panel, wcol * (WB * BS), WB * BS, 0)
            term = local_product(block_values[arow, wcol], block_rows[arow, wcol], block_cols[arow, wcol], block_count[arow, wcol], wide, AB, False)
            current = lax.dynamic_slice_in_dim(total, arow * (AB * BS), AB * BS, 0)
            return lax.dynamic_update_slice_in_dim(total, current + rounded(term), arow * (AB * BS), 0)
        field_y = lax.fori_loop(jnp.int32(0), jnp.int32(devices_all), author_step, jnp.zeros((authors, PANEL), jnp.float32))
        author_basis = orthonormal(field_y, authors)

        def word_step(index, total):
            arow = index // N_WORD
            wcol = index % N_WORD
            basis_rows = lax.dynamic_slice_in_dim(author_basis, arow * (AB * BS), AB * BS, 0)
            term = local_product(block_values[arow, wcol], block_rows[arow, wcol], block_cols[arow, wcol], block_count[arow, wcol], basis_rows, WB, True)
            current = lax.dynamic_slice_in_dim(total, wcol * (WB * BS), WB * BS, 0)
            return lax.dynamic_update_slice_in_dim(total, current + rounded(term), wcol * (WB * BS), 0)
        field_z = lax.fori_loop(jnp.int32(0), jnp.int32(devices_all), word_step, jnp.zeros((words, PANEL), jnp.float32))
        panel = orthonormal(field_z, words)
    return (author_basis, panel)
```

```python
import functools
import jax
import jax.numpy as jnp
from jax import lax
from jax.experimental import pallas as pl
from jax.experimental.pallas import tpu as pltpu
from jax.sharding import PartitionSpec as P

ITERS = 2
GROUP = 4
SLOTS = 16
HIGH = lax.Precision.HIGHEST


def product_kernel(src_ids, dst_ids, count, values, panel, out, total, *, transpose):
    step = pl.program_id(0)
    size = values.shape[1]
    blocks = out.shape[0] // size

    @pl.when(step == 0)
    def _():
        def clear(index, carry):
            total[index] = jnp.zeros_like(total[index])
            return carry

        lax.fori_loop(0, blocks, clear, 0)

    def group(index, carry):
        base = step * SLOTS + index * GROUP
        prods = []
        for offset in range(GROUP):
            part = values[index * GROUP + offset]
            source = panel[pl.ds(pl.multiple_of(src_ids[base + offset] * size, size), size), :]
            dims = (((0,), (0,)), ((), ())) if transpose else (((1,), (0,)), ((), ()))
            prods.append(lax.dot_general(part, source, dims, preferred_element_type=jnp.float32))
        for offset in range(GROUP):
            total[dst_ids[base + offset]] += prods[offset]
        return carry

    live = jnp.clip(count[0] - step * SLOTS, 0, SLOTS)
    lax.fori_loop(0, (live + GROUP - 1) // GROUP, group, 0)

    @pl.when(step == pl.num_programs(0) - 1)
    def _():
        def emit(index, carry):
            out[pl.ds(pl.multiple_of(index * size, size), size), :] = total[index].astype(out.dtype)
            return carry

        lax.fori_loop(0, blocks, emit, 0)


def product(values, src_ids, dst_ids, count, panel, out_blocks, transpose):
    cap, size, _ = values.shape
    width = panel.shape[1]
    dst_ids = jnp.where(jnp.arange(cap, dtype=jnp.int32) < count, dst_ids, out_blocks)
    return pl.pallas_call(
        functools.partial(product_kernel, transpose=transpose),
        out_shape=jax.ShapeDtypeStruct((out_blocks * size, width), jnp.bfloat16),
        grid_spec=pltpu.PrefetchScalarGridSpec(
            num_scalar_prefetch=3,
            grid=(cap // SLOTS,),
            in_specs=[
                pl.BlockSpec((SLOTS, size, size), lambda i, *_: (i, 0, 0)),
                pl.BlockSpec(panel.shape, lambda i, *_: (0, 0), pipeline_mode=pl.Buffered(1)),
            ],
            out_specs=pl.BlockSpec((out_blocks * size, width), lambda i, *_: (0, 0), pipeline_mode=pl.Buffered(1)),
            scratch_shapes=[pltpu.VMEM((out_blocks + 1, size, width), jnp.float32)],
        ),
        compiler_params=pltpu.CompilerParams(vmem_limit_bytes=52 * 1024 * 1024),
        cost_estimate=pl.CostEstimate(
            flops=2 * cap * size * size * width,
            bytes_accessed=2 * (cap * size * size + panel.size + out_blocks * size * width),
            transcendentals=0,
        ),
        name="product_t" if transpose else "product",
    )(src_ids, dst_ids, count.reshape(1), values, panel)


def gram_of(field):
    return lax.dot_general(
        field, field, (((0,), (0,)), ((), ())), precision=HIGH, preferred_element_type=jnp.float32
    )


def hop_core(array):
    return lax.ppermute(array, "author", [(i, i ^ 1) for i in range(8)])


def hop_x(array, k):
    return lax.ppermute(array, "author", [(i, (i + 2 * k) % 8) for i in range(8)])


def hop_y(array, k):
    return lax.ppermute(array, "word", [(i, (i + 4 * k) % 16) for i in range(16)])


def hop_z(array, k):
    return lax.ppermute(array, "word", [(i, (i // 4) * 4 + (i + k) % 4) for i in range(16)])


def pick(array, index):
    return lax.dynamic_index_in_dim(array, index, 0, keepdims=False)


def split_core(gram, core):
    halves = gram.reshape(2, gram.shape[0] // 2, gram.shape[1])
    return pick(halves, core) + hop_core(pick(halves, 1 - core))


def join_core(half, core):
    other = hop_core(half)
    return jnp.where(core == 0, jnp.concatenate([half, other]), jnp.concatenate([other, half]))


def sum_author(gram):
    core = lax.axis_index("author") % 2
    half = split_core(gram, core)
    parts = [hop_x(half, k) for k in (1, 3, 2)]
    half = (half + parts[2]) + (parts[0] + parts[1])
    return join_core(half, core)


def sum_all(gram):
    place = lax.axis_index("author")
    core, x = place % 2, place // 2
    half = split_core(gram, core)
    chunks = half.reshape(4, half.shape[0] // 4, half.shape[1])
    got = [hop_x(pick(chunks, (x + k) % 4), k) for k in (1, 3, 2)]
    part = (pick(chunks, x) + got[2]) + (got[0] + got[1])
    for hop in (hop_y, hop_z):
        got = [hop(part, k) for k in (1, 3, 2)]
        part = (part + got[2]) + (got[0] + got[1])
    ring = jnp.stack([part] + [hop_x(part, k) for k in (1, 2, 3)])
    half = jnp.take(ring, (x - jnp.arange(4)) % 4, axis=0).reshape(half.shape)
    return join_core(half, core)


def whitener(gram):
    lower = jnp.linalg.cholesky(gram)
    inverse = jax.scipy.linalg.solve_triangular(
        lower, jnp.eye(gram.shape[0], dtype=jnp.float32), lower=True
    )
    return inverse.T


def apply(field, factor):
    return jnp.dot(field, factor, precision=HIGH, preferred_element_type=jnp.float32)


def scatter_word(terms):
    parts = lax.all_to_all(terms.reshape(16, -1, terms.shape[1]), "word", 0, 0)
    return jnp.sum(parts.astype(jnp.float32), axis=0)


def gather_word(share):
    copies = jnp.broadcast_to(share[None], (16,) + share.shape)
    return lax.all_to_all(copies, "word", 0, 0).reshape(-1, share.shape[1])


def shards(block_values, block_rows, block_cols, block_count, omega):
    values = block_values[0, 0]
    rows = block_rows[0, 0]
    cols = block_cols[0, 0]
    count = block_count[0, 0]
    size = values.shape[1]
    word_blocks = omega.shape[0] // size
    author_blocks = 32
    authors = author_blocks * size * lax.axis_size("author")
    words = word_blocks * size * lax.axis_size("word")
    wide = omega
    word_factor = None
    for turn in range(ITERS):
        terms = product(values, cols, rows, count, wide, author_blocks, False)
        y = scatter_word(terms)
        if word_factor is not None:
            y = apply(y, word_factor)
        y_rows = gather_word(y.astype(jnp.bfloat16))
        author_factor = whitener(
            sum_author(lax.dot_general(y_rows, y_rows, (((0,), (0,)), ((), ())), preferred_element_type=jnp.float32))
            / authors
        )
        terms = product(values, rows, cols, count, y_rows, word_blocks, True)
        z = lax.psum_scatter(terms, "author", scatter_dimension=0, tiled=True).astype(jnp.float32)
        z = apply(z, author_factor)
        word_factor = whitener(sum_all(gram_of(z)) / words)
        if turn + 1 < ITERS:
            wide = lax.all_gather(z.astype(jnp.bfloat16), "author", axis=0, tiled=True)
    author_basis = apply(y, author_factor).astype(jnp.bfloat16)
    word_basis = apply(z, word_factor).astype(jnp.bfloat16)
    return (author_basis, word_basis)


def solution(mesh):
    return jax.shard_map(
        shards,
        mesh=mesh,
        in_specs=(
            P("author", "word", None, None, None),
            P("author", "word", None),
            P("author", "word", None),
            P("author", "word"),
            P("word", None),
        ),
        out_specs=(P(("author", "word"), None), P(("word", "author"), None)),
        check_vma=False,
    )
```

```python
import jax
import jax.numpy as jnp
from jax import lax
from jax.experimental import pallas as pl
from jax.experimental.pallas import tpu as pltpu
from jax.sharding import PartitionSpec as P

ITERS = 2
GROUP = 4
AHEAD = 8
BLOCK = 64
HIGH = lax.Precision.HIGHEST


def product_kernel(src_ids, dst_ids, count, values, panel, out, total, part, source, part_sem, source_sem):
    size = part.shape[1]
    groups = (count[0] + GROUP - 1) // GROUP

    def copies(group):
        first = group * GROUP
        yield pltpu.make_async_copy(
            values.at[pl.ds(first, GROUP)], part.at[pl.ds(first, GROUP)], part_sem.at[group]
        )
        for offset in range(GROUP):
            slot = first + offset
            rows = pl.ds(pl.multiple_of(src_ids[slot] * size, size), size)
            yield pltpu.make_async_copy(panel.at[rows], source.at[slot], source_sem.at[slot])

    def start(group, carry):
        for copy in copies(group):
            copy.start()
        return carry

    def clear(index, carry):
        total[index] = jnp.zeros_like(total[index])
        return carry

    def work(group, carry):
        @pl.when(group + AHEAD < groups)
        def _():
            start(group + AHEAD, 0)

        for copy in copies(group):
            copy.wait()
        first = group * GROUP
        prods = [
            jnp.dot(part[first + offset], source[first + offset], preferred_element_type=jnp.float32)
            for offset in range(GROUP)
        ]
        for offset in range(GROUP):
            total[dst_ids[first + offset]] += prods[offset]
        return carry

    def emit(index, carry):
        out[pl.ds(pl.multiple_of(index * size, size), size), :] = total[index].astype(out.dtype)
        return carry

    lax.fori_loop(0, jnp.minimum(AHEAD, groups), start, 0)
    lax.fori_loop(0, total.shape[0], clear, 0)
    lax.fori_loop(0, groups, work, 0)
    lax.fori_loop(0, out.shape[0] // size, emit, 0)


def product_t_kernel(src_ids, dst_ids, count, values, panel, out, total, part, staged, part_sem, out_sem):
    size = part.shape[1]
    groups = (count[0] + GROUP - 1) // GROUP

    def fetch(group):
        span = pl.ds(group * GROUP, GROUP)
        return pltpu.make_async_copy(values.at[span], part.at[span], part_sem.at[group])

    def start(group, carry):
        fetch(group).start()
        return carry

    def clear(index, carry):
        total[index] = jnp.zeros_like(total[index])
        return carry

    def work(group, carry):
        fetch(group).wait()
        first = group * GROUP
        prods = []
        for offset in range(GROUP):
            rows = pl.ds(pl.multiple_of(src_ids[first + offset] * size, size), size)
            prods.append(
                lax.dot_general(
                    part[first + offset],
                    panel[rows, :],
                    (((0,), (0,)), ((), ())),
                    preferred_element_type=jnp.float32,
                )
            )
        for offset in range(GROUP):
            total[dst_ids[first + offset]] += prods[offset]
        return carry

    def emit(index, carry):
        staged[pl.ds(pl.multiple_of(index * size, size), size), :] = total[index].astype(staged.dtype)
        return carry

    lax.fori_loop(0, groups, start, 0)
    lax.fori_loop(0, total.shape[0], clear, 0)
    lax.fori_loop(0, groups, work, 0)
    blocks = out.shape[0] // size
    pieces = out_sem.shape[0]
    sends = []
    for piece in range(pieces):
        lax.fori_loop(piece * blocks // pieces, (piece + 1) * blocks // pieces, emit, 0)
        rows = pl.ds(piece * out.shape[0] // pieces, out.shape[0] // pieces)
        sends.append(pltpu.make_async_copy(staged.at[rows], out.at[rows], out_sem.at[piece]))
        sends[-1].start()
    for send in sends:
        send.wait()


def product(values, src_ids, dst_ids, count, panel, out_blocks, transpose):
    cap, size, _ = values.shape
    width = panel.shape[1]
    dst_ids = jnp.where(jnp.arange(cap, dtype=jnp.int32) < count, dst_ids, out_blocks)
    smem = pl.BlockSpec(memory_space=pltpu.SMEM)
    vmem = pl.BlockSpec(memory_space=pltpu.VMEM)
    whole = pl.BlockSpec(memory_space=pl.ANY)
    values = pltpu.with_memory_space_constraint(values, pltpu.HBM)
    rows = out_blocks * size
    scratch = [
        pltpu.VMEM((out_blocks + 1, size, width), jnp.float32),
        pltpu.VMEM((cap, size, size), values.dtype),
    ]
    if transpose:
        kernel, panel_spec, out_spec = product_t_kernel, vmem, whole
        out_shape = jax.ShapeDtypeStruct((rows, width), jnp.bfloat16)
        scratch += [pltpu.VMEM((rows, width), jnp.bfloat16)]
        scratch += [pltpu.SemaphoreType.DMA((cap // GROUP,)), pltpu.SemaphoreType.DMA((8,))]
    else:
        kernel, panel_spec, out_spec = product_kernel, whole, vmem
        panel = pltpu.with_memory_space_constraint(panel, pltpu.HBM)
        out_shape = pltpu.VMEM((rows, width), jnp.bfloat16)
        scratch += [pltpu.VMEM((cap, size, width), panel.dtype)]
        scratch += [pltpu.SemaphoreType.DMA((cap // GROUP,)), pltpu.SemaphoreType.DMA((cap,))]
    return pl.pallas_call(
        kernel,
        out_shape=out_shape,
        in_specs=[smem, smem, smem, whole, panel_spec],
        out_specs=out_spec,
        scratch_shapes=scratch,
        compiler_params=pltpu.CompilerParams(vmem_limit_bytes=36 * 1024 * 1024),
        cost_estimate=pl.CostEstimate(
            flops=2 * cap * size * size * width,
            bytes_accessed=2 * (cap * size * size + panel.size + rows * width),
            transcendentals=0,
        ),
        name="product_t" if transpose else "product",
    )(src_ids, dst_ids, count.reshape(1), values, panel)


def fold_kernel(parts, factor, field, copies):
    total = parts[0].astype(jnp.float32)
    for index in range(1, parts.shape[0]):
        total += parts[index].astype(jnp.float32)
    if factor is not None:
        total = apply_t(total, factor[...])
    field[...] = total
    short = total.astype(copies.dtype)
    for index in range(copies.shape[0]):
        copies[index] = short


def fold(parts, factor):
    vmem = pl.BlockSpec(memory_space=pltpu.VMEM)
    operands = (parts,) if factor is None else (parts, factor)
    kernel = fold_kernel if factor is not None else lambda p, f, c: fold_kernel(p, None, f, c)
    return pl.pallas_call(
        kernel,
        out_shape=(
            pltpu.VMEM(parts.shape[1:], jnp.float32),
            pltpu.VMEM(parts.shape, jnp.bfloat16),
        ),
        in_specs=[vmem] * len(operands),
        out_specs=(vmem, vmem),
        name="fold",
    )(*operands)


def gram_of(field):
    return lax.dot_general(
        field, field, (((0,), (0,)), ((), ())), precision=HIGH, preferred_element_type=jnp.float32
    )


def hop_core(array):
    return lax.ppermute(array, "author", [(i, i ^ 1) for i in range(8)])


def hop_x(array, k):
    return lax.ppermute(array, "author", [(i, (i + 2 * k) % 8) for i in range(8)])


def hop_y(array, k):
    return lax.ppermute(array, "word", [(i, (i + 4 * k) % 16) for i in range(16)])


def hop_z(array, k):
    return lax.ppermute(array, "word", [(i, (i // 4) * 4 + (i + k) % 4) for i in range(16)])


def pick(array, index):
    return lax.dynamic_index_in_dim(array, index, 0, keepdims=False)


def split_core(gram, core):
    halves = gram.reshape(2, gram.shape[0] // 2, gram.shape[1])
    return pick(halves, core) + hop_core(pick(halves, 1 - core))


def join_core(half, core):
    other = hop_core(half)
    return jnp.where(core == 0, jnp.concatenate([half, other]), jnp.concatenate([other, half]))


def sum_author(gram):
    core = lax.axis_index("author") % 2
    half = split_core(gram, core)
    parts = [hop_x(half, k) for k in (1, 3, 2)]
    half = (half + parts[2]) + (parts[0] + parts[1])
    return join_core(half, core)


def sum_all(gram):
    place = lax.axis_index("author")
    core, x = place % 2, place // 2
    half = split_core(gram, core)
    chunks = half.reshape(4, half.shape[0] // 4, half.shape[1])
    got = [hop_x(pick(chunks, (x + k) % 4), k) for k in (1, 3, 2)]
    part = (pick(chunks, x) + got[2]) + (got[0] + got[1])
    for hop in (hop_y, hop_z):
        got = [hop(part, k) for k in (1, 3, 2)]
        part = (part + got[2]) + (got[0] + got[1])
    ring = jnp.stack([part] + [hop_x(part, k) for k in (1, 2, 3)])
    half = jnp.take(ring, (x - jnp.arange(4)) % 4, axis=0).reshape(half.shape)
    return join_core(half, core)


def eliminate(strips):
    shape = strips[0].shape
    sub = lax.broadcasted_iota(jnp.int32, shape, 0)
    half = shape[1] // 2

    def column(strip, lane):
        return jnp.broadcast_to(strip[:, lane : lane + 1], shape)

    def row(strip, j):
        return jnp.broadcast_to(strip[j : j + 1, :], shape)

    for p in range(len(strips)):
        lead = strips[p]
        lanes = [half + 8 * p + j for j in range(8)]
        cols = [column(lead, lane) for lane in lanes]
        below = {i: [column(strips[i], lane) for lane in lanes] for i in range(p + 1, len(strips))}
        scale = jnp.zeros(shape, jnp.float32)
        for j in range(0, 8, 2):
            a, b, c = row(cols[j], j), row(cols[j + 1], j), row(cols[j + 1], j + 1)
            inv0 = 1.0 / a
            inv1 = a / (a * c - b * b)
            m0 = jnp.where(sub > j, cols[j] * inv0, 0.0)
            m1 = jnp.where(sub > j + 1, (cols[j + 1] - m0 * b) * inv1, 0.0)
            top0 = row(lead, j)
            top1 = row(lead, j + 1) - (b * inv0) * top0
            lead = (lead - m0 * top0) - m1 * top1
            scale = jnp.where(sub == j, lax.rsqrt(a), scale)
            scale = jnp.where(sub == j + 1, jnp.sqrt(inv1), scale)
            tops = []
            for k in range(j + 2, 8):
                u0 = row(cols[k], j)
                u1 = row(cols[k], j + 1) - (b * inv0) * u0
                cols[k] = (cols[k] - m0 * u0) - m1 * u1
                tops.append((u0, u1))
            for i, col in below.items():
                n0 = col[j] * inv0
                n1 = (col[j + 1] - n0 * b) * inv1
                for k, (u0, u1) in zip(range(j + 2, 8), tops):
                    col[k] = (col[k] - n0 * u0) - n1 * u1
                strips[i] = (strips[i] - n0 * top0) - n1 * top1
        strips[p] = lead * scale
    return strips


def whiten_kernel(g_ref, out_ref, s_ref, y_ref):
    n = g_ref.shape[0]
    g = g_ref[...]
    eye = lax.broadcasted_iota(jnp.int32, (n, n), 0) == lax.broadcasted_iota(jnp.int32, (n, n), 1)
    diag = jnp.where(eye, g, 0.0)
    across = lax.rsqrt(jnp.sum(diag, axis=0, keepdims=True))
    down = lax.rsqrt(jnp.sum(diag, axis=1, keepdims=True))
    s_ref[...] = g * across * down
    y_ref[...] = jnp.where(eye, 1.0, 0.0)
    lane = lax.broadcasted_iota(jnp.int32, (BLOCK, n), 1)
    def stage(at, carry):
        rows = pl.ds(pl.multiple_of(at * BLOCK, BLOCK), BLOCK)
        left, right = s_ref[rows, :], y_ref[rows, :]
        turned = pltpu.roll(left, lax.rem(n + BLOCK - at * BLOCK, n), 1)[:, : 2 * BLOCK]
        i0 = lax.broadcasted_iota(jnp.int32, turned.shape, 0)
        i1 = lax.broadcasted_iota(jnp.int32, turned.shape, 1)
        start = jnp.where(i1 < BLOCK, jnp.where(i0 == i1, 1.0, 0.0), turned)
        strips = eliminate([start[8 * i : 8 * i + 8] for i in range(BLOCK // 8)])
        inverse = jnp.concatenate(strips, axis=0)[:, :BLOCK]
        dot = lambda u, v, d: lax.dot_general(u, v, (((d,), (0,)), ((), ())), precision=HIGH, preferred_element_type=jnp.float32)
        left = dot(inverse, left, 1)
        right = dot(inverse, right, 1)
        rest = jnp.where(lane >= (at + 1) * BLOCK, left, 0.0)
        s_ref[...] -= dot(rest, left, 0)
        y_ref[...] -= dot(rest, right, 0)
        y_ref[rows, :] = right
        return carry
    lax.fori_loop(0, n // BLOCK, stage, 0)
    out_ref[...] = y_ref[...] * across


def whitener(gram):
    return pl.pallas_call(
        whiten_kernel,
        out_shape=jax.ShapeDtypeStruct(gram.shape, jnp.float32),
        scratch_shapes=[pltpu.VMEM(gram.shape, jnp.float32)] * 2,
        cost_estimate=pl.CostEstimate(flops=10**9, bytes_accessed=40 * 10**6, transcendentals=0),
        name="whitener",
    )(gram)


def apply_t(field, inverse):
    return lax.dot_general(
        field, inverse, (((1,), (1,)), ((), ())), precision=HIGH, preferred_element_type=jnp.float32
    )


def swap_word(parts):
    return lax.all_to_all(parts, "word", 0, 0)


def shards(block_values, block_rows, block_cols, block_count, omega):
    values = block_values[0, 0]
    rows = block_rows[0, 0]
    cols = block_cols[0, 0]
    count = block_count[0, 0]
    size = values.shape[1]
    word_blocks = omega.shape[0] // size
    author_blocks = 32
    authors = author_blocks * size * lax.axis_size("author")
    words = word_blocks * size * lax.axis_size("word")
    wide = omega
    word_factor = None
    for turn in range(ITERS):
        terms = product(values, cols, rows, count, wide, author_blocks, False)
        y, copies = fold(swap_word(terms.reshape(16, -1, terms.shape[1])), word_factor)
        y_rows = swap_word(copies).reshape(terms.shape)
        author_factor = whitener(
            sum_author(lax.dot_general(y_rows, y_rows, (((0,), (0,)), ((), ())), preferred_element_type=jnp.float32))
            / authors
        )
        terms = product(values, rows, cols, count, y_rows, word_blocks, True)
        z = lax.psum_scatter(terms, "author", scatter_dimension=0, tiled=True).astype(jnp.float32)
        z = apply_t(z, author_factor)
        word_factor = whitener(sum_all(gram_of(z)) / words)
        if turn + 1 < ITERS:
            wide = lax.all_gather(z.astype(jnp.bfloat16), "author", axis=0, tiled=True)
    author_basis = apply_t(y, author_factor).astype(jnp.bfloat16)
    word_basis = apply_t(z, word_factor).astype(jnp.bfloat16)
    return (author_basis, word_basis)


def solution(mesh):
    return jax.shard_map(
        shards,
        mesh=mesh,
        in_specs=(
            P("author", "word", None, None, None),
            P("author", "word", None),
            P("author", "word", None),
            P("author", "word"),
            P("word", None),
        ),
        out_specs=(P(("author", "word"), None), P(("word", "author"), None)),
        check_vma=False,
    )
```

```python
import jax
import jax.numpy as jnp
from jax import lax
from jax.experimental import pallas as pl
from jax.experimental.pallas import tpu as pltpu
from jax.sharding import PartitionSpec as P

ITERS = 2
GROUP = 4
AHEAD = 8
BLOCK = 64
HIGH = lax.Precision.HIGHEST


def product_kernel(src_ids, dst_ids, count, values, panel, out, total, part, source, part_sem, source_sem):
    size = part.shape[1]
    groups = (count[0] + GROUP - 1) // GROUP

    def copies(group):
        first = group * GROUP
        yield pltpu.make_async_copy(
            values.at[pl.ds(first, GROUP)], part.at[pl.ds(first, GROUP)], part_sem.at[group]
        )
        for offset in range(GROUP):
            slot = first + offset
            rows = pl.ds(pl.multiple_of(src_ids[slot] * size, size), size)
            yield pltpu.make_async_copy(panel.at[rows], source.at[slot], source_sem.at[slot])

    def start(group, carry):
        for copy in copies(group):
            copy.start()
        return carry

    def clear(index, carry):
        total[index] = jnp.zeros_like(total[index])
        return carry

    def work(group, carry):
        @pl.when(group + AHEAD < groups)
        def _():
            start(group + AHEAD, 0)

        for copy in copies(group):
            copy.wait()
        first = group * GROUP
        prods = [
            jnp.dot(part[first + offset], source[first + offset], preferred_element_type=jnp.float32)
            for offset in range(GROUP)
        ]
        for offset in range(GROUP):
            total[dst_ids[first + offset]] += prods[offset]
        return carry

    def emit(index, carry):
        out[pl.ds(pl.multiple_of(index * size, size), size), :] = total[index].astype(out.dtype)
        return carry

    lax.fori_loop(0, jnp.minimum(AHEAD, groups), start, 0)
    lax.fori_loop(0, total.shape[0], clear, 0)
    lax.fori_loop(0, groups, work, 0)
    lax.fori_loop(0, out.shape[0] // size, emit, 0)


def product_t_kernel(src_ids, dst_ids, count, values, panel, out, total, part, staged, part_sem, out_sem):
    size = part.shape[1]
    groups = (count[0] + GROUP - 1) // GROUP

    def fetch(group):
        span = pl.ds(group * GROUP, GROUP)
        return pltpu.make_async_copy(values.at[span], part.at[span], part_sem.at[group])

    def start(group, carry):
        fetch(group).start()
        return carry

    def clear(index, carry):
        total[index] = jnp.zeros_like(total[index])
        return carry

    def work(group, carry):
        fetch(group).wait()
        first = group * GROUP
        prods = []
        for offset in range(GROUP):
            rows = pl.ds(pl.multiple_of(src_ids[first + offset] * size, size), size)
            prods.append(
                lax.dot_general(
                    part[first + offset],
                    panel[rows, :],
                    (((0,), (0,)), ((), ())),
                    preferred_element_type=jnp.float32,
                )
            )
        for offset in range(GROUP):
            total[dst_ids[first + offset]] += prods[offset]
        return carry

    def emit(index, carry):
        staged[pl.ds(pl.multiple_of(index * size, size), size), :] = total[index].astype(staged.dtype)
        return carry

    lax.fori_loop(0, groups, start, 0)
    lax.fori_loop(0, total.shape[0], clear, 0)
    lax.fori_loop(0, groups, work, 0)
    blocks = out.shape[0] // size
    pieces = out_sem.shape[0]
    sends = []
    for piece in range(pieces):
        lax.fori_loop(piece * blocks // pieces, (piece + 1) * blocks // pieces, emit, 0)
        rows = pl.ds(piece * out.shape[0] // pieces, out.shape[0] // pieces)
        sends.append(pltpu.make_async_copy(staged.at[rows], out.at[rows], out_sem.at[piece]))
        sends[-1].start()
    for send in sends:
        send.wait()


def product(values, src_ids, dst_ids, count, panel, out_blocks, transpose):
    cap, size, _ = values.shape
    width = panel.shape[1]
    dst_ids = jnp.where(jnp.arange(cap, dtype=jnp.int32) < count, dst_ids, out_blocks)
    smem = pl.BlockSpec(memory_space=pltpu.SMEM)
    vmem = pl.BlockSpec(memory_space=pltpu.VMEM)
    whole = pl.BlockSpec(memory_space=pl.ANY)
    values = pltpu.with_memory_space_constraint(values, pltpu.HBM)
    rows = out_blocks * size
    scratch = [
        pltpu.VMEM((out_blocks + 1, size, width), jnp.float32),
        pltpu.VMEM((cap, size, size), values.dtype),
    ]
    if transpose:
        kernel, panel_spec, out_spec = product_t_kernel, vmem, whole
        out_shape = jax.ShapeDtypeStruct((rows, width), jnp.bfloat16)
        scratch += [pltpu.VMEM((rows, width), jnp.bfloat16)]
        scratch += [pltpu.SemaphoreType.DMA((cap // GROUP,)), pltpu.SemaphoreType.DMA((8,))]
    else:
        kernel, panel_spec, out_spec = product_kernel, whole, vmem
        panel = pltpu.with_memory_space_constraint(panel, pltpu.HBM)
        out_shape = pltpu.VMEM((rows, width), jnp.bfloat16)
        scratch += [pltpu.VMEM((cap, size, width), panel.dtype)]
        scratch += [pltpu.SemaphoreType.DMA((cap // GROUP,)), pltpu.SemaphoreType.DMA((cap,))]
    return pl.pallas_call(
        kernel,
        out_shape=out_shape,
        in_specs=[smem, smem, smem, whole, panel_spec],
        out_specs=out_spec,
        scratch_shapes=scratch,
        compiler_params=pltpu.CompilerParams(vmem_limit_bytes=36 * 1024 * 1024),
        cost_estimate=pl.CostEstimate(
            flops=2 * cap * size * size * width,
            bytes_accessed=2 * (cap * size * size + panel.size + rows * width),
            transcendentals=0,
        ),
        name="product_t" if transpose else "product",
    )(src_ids, dst_ids, count.reshape(1), values, panel)


def fold_kernel(parts, factor, field, copies):
    total = parts[0].astype(jnp.float32)
    for index in range(1, parts.shape[0]):
        total += parts[index].astype(jnp.float32)
    if factor is not None:
        total = apply_t(total, factor[...])
    field[...] = total
    short = total.astype(copies.dtype)
    for index in range(copies.shape[0]):
        copies[index] = short


def fold(parts, factor):
    vmem = pl.BlockSpec(memory_space=pltpu.VMEM)
    operands = (parts,) if factor is None else (parts, factor)
    kernel = fold_kernel if factor is not None else lambda p, f, c: fold_kernel(p, None, f, c)
    return pl.pallas_call(
        kernel,
        out_shape=(
            pltpu.VMEM(parts.shape[1:], jnp.float32),
            pltpu.VMEM(parts.shape, jnp.bfloat16),
        ),
        in_specs=[vmem] * len(operands),
        out_specs=(vmem, vmem),
        name="fold",
    )(*operands)


def gram_of(field):
    return lax.dot_general(
        field, field, (((0,), (0,)), ((), ())), precision=HIGH, preferred_element_type=jnp.float32
    )


def hop_core(array):
    return lax.ppermute(array, "author", [(i, i ^ 1) for i in range(8)])


def hop_x(array, k):
    return lax.ppermute(array, "author", [(i, (i + 2 * k) % 8) for i in range(8)])


def hop_y(array, k):
    return lax.ppermute(array, "word", [(i, (i + 4 * k) % 16) for i in range(16)])


def hop_z(array, k):
    return lax.ppermute(array, "word", [(i, (i // 4) * 4 + (i + k) % 4) for i in range(16)])


def pick(array, index):
    return lax.dynamic_index_in_dim(array, index, 0, keepdims=False)


def split_core(gram, core):
    halves = gram.reshape(2, gram.shape[0] // 2, gram.shape[1])
    return pick(halves, core) + hop_core(pick(halves, 1 - core))


def join_core(half, core):
    other = hop_core(half)
    return jnp.where(core == 0, jnp.concatenate([half, other]), jnp.concatenate([other, half]))


def sum_author(gram):
    core = lax.axis_index("author") % 2
    half = split_core(gram, core)
    parts = [hop_x(half, k) for k in (1, 3, 2)]
    half = (half + parts[2]) + (parts[0] + parts[1])
    return join_core(half, core)


def sum_all(gram):
    place = lax.axis_index("author")
    core, x = place % 2, place // 2
    half = split_core(gram, core)
    chunks = half.reshape(4, half.shape[0] // 4, half.shape[1])
    got = [hop_x(pick(chunks, (x + k) % 4), k) for k in (1, 3, 2)]
    part = (pick(chunks, x) + got[2]) + (got[0] + got[1])
    for hop in (hop_y, hop_z):
        got = [hop(part, k) for k in (1, 3, 2)]
        part = (part + got[2]) + (got[0] + got[1])
    ring = jnp.stack([part] + [hop_x(part, k) for k in (1, 2, 3)])
    half = jnp.take(ring, (x - jnp.arange(4)) % 4, axis=0).reshape(half.shape)
    return join_core(half, core)


def eliminate(strips):
    shape = strips[0].shape
    sub = lax.broadcasted_iota(jnp.int32, shape, 0)
    half = shape[1] // 2

    def column(strip, lane):
        return jnp.broadcast_to(strip[:, lane : lane + 1], shape)

    def row(strip, j):
        return jnp.broadcast_to(strip[j : j + 1, :], shape)

    for p in range(len(strips)):
        lead = strips[p]
        lanes = [half + 8 * p + j for j in range(8)]
        cols = [column(lead, lane) for lane in lanes]
        below = {i: [column(strips[i], lane) for lane in lanes] for i in range(p + 1, len(strips))}
        scale = jnp.zeros(shape, jnp.float32)
        for j in range(0, 8, 2):
            a, b, c = row(cols[j], j), row(cols[j + 1], j), row(cols[j + 1], j + 1)
            inv0 = 1.0 / a
            inv1 = a / (a * c - b * b)
            m0 = jnp.where(sub > j, cols[j] * inv0, 0.0)
            m1 = jnp.where(sub > j + 1, (cols[j + 1] - m0 * b) * inv1, 0.0)
            top0 = row(lead, j)
            top1 = row(lead, j + 1) - (b * inv0) * top0
            lead = (lead - m0 * top0) - m1 * top1
            scale = jnp.where(sub == j, lax.rsqrt(a), scale)
            scale = jnp.where(sub == j + 1, jnp.sqrt(inv1), scale)
            tops = []
            for k in range(j + 2, 8):
                u0 = row(cols[k], j)
                u1 = row(cols[k], j + 1) - (b * inv0) * u0
                cols[k] = (cols[k] - m0 * u0) - m1 * u1
                tops.append((u0, u1))
            for i, col in below.items():
                n0 = col[j] * inv0
                n1 = (col[j + 1] - n0 * b) * inv1
                for k, (u0, u1) in zip(range(j + 2, 8), tops):
                    col[k] = (col[k] - n0 * u0) - n1 * u1
                strips[i] = (strips[i] - n0 * top0) - n1 * top1
        strips[p] = lead * scale
    return strips


def whiten_kernel(g_ref, out_ref, s_ref, y_ref):
    n = g_ref.shape[0]
    g = g_ref[...]
    eye = lax.broadcasted_iota(jnp.int32, (n, n), 0) == lax.broadcasted_iota(jnp.int32, (n, n), 1)
    diag = jnp.where(eye, g, 0.0)
    across = lax.rsqrt(jnp.sum(diag, axis=0, keepdims=True))
    down = lax.rsqrt(jnp.sum(diag, axis=1, keepdims=True))
    s_ref[...] = g * across * down
    y_ref[...] = jnp.where(eye, 1.0, 0.0)
    lane = lax.broadcasted_iota(jnp.int32, (BLOCK, n), 1)
    def stage(at, carry):
        rows = pl.ds(pl.multiple_of(at * BLOCK, BLOCK), BLOCK)
        left, right = s_ref[rows, :], y_ref[rows, :]
        turned = pltpu.roll(left, lax.rem(n + BLOCK - at * BLOCK, n), 1)[:, : 2 * BLOCK]
        i0 = lax.broadcasted_iota(jnp.int32, turned.shape, 0)
        i1 = lax.broadcasted_iota(jnp.int32, turned.shape, 1)
        start = jnp.where(i1 < BLOCK, jnp.where(i0 == i1, 1.0, 0.0), turned)
        strips = eliminate([start[8 * i : 8 * i + 8] for i in range(BLOCK // 8)])
        inverse = jnp.concatenate(strips, axis=0)[:, :BLOCK]
        dot = lambda u, v, d: lax.dot_general(u, v, (((d,), (0,)), ((), ())), precision=HIGH, preferred_element_type=jnp.float32)
        left = dot(inverse, left, 1)
        right = dot(inverse, right, 1)
        rest = jnp.where(lane >= (at + 1) * BLOCK, left, 0.0)
        s_ref[...] -= dot(rest, left, 0)
        y_ref[...] -= dot(rest, right, 0)
        y_ref[rows, :] = right
        return carry
    lax.fori_loop(0, n // BLOCK, stage, 0)
    out_ref[...] = y_ref[...] * across


def whitener(gram):
    return pl.pallas_call(
        whiten_kernel,
        out_shape=jax.ShapeDtypeStruct(gram.shape, jnp.float32),
        scratch_shapes=[pltpu.VMEM(gram.shape, jnp.float32)] * 2,
        cost_estimate=pl.CostEstimate(flops=10**9, bytes_accessed=40 * 10**6, transcendentals=0),
        name="whitener",
    )(gram)


def apply_t(field, inverse):
    return lax.dot_general(
        field, inverse, (((1,), (1,)), ((), ())), precision=HIGH, preferred_element_type=jnp.float32
    )


def swap_word(parts):
    return lax.all_to_all(parts, "word", 0, 0)


def shards(block_values, block_rows, block_cols, block_count, omega):
    values = block_values[0, 0]
    rows = block_rows[0, 0]
    cols = block_cols[0, 0]
    count = block_count[0, 0]
    size = values.shape[1]
    word_blocks = omega.shape[0] // size
    author_blocks = 32
    authors = author_blocks * size * lax.axis_size("author")
    words = word_blocks * size * lax.axis_size("word")
    wide = omega
    word_factor = None
    for turn in range(ITERS):
        terms = product(values, cols, rows, count, wide, author_blocks, False)
        y, copies = fold(swap_word(terms.reshape(16, -1, terms.shape[1])), word_factor)
        y_rows = swap_word(copies).reshape(terms.shape)
        author_factor = whitener(
            sum_author(lax.dot_general(y_rows, y_rows, (((0,), (0,)), ((), ())), preferred_element_type=jnp.float32))
            / authors
        )
        terms = product(values, rows, cols, count, y_rows, word_blocks, True)
        z = lax.psum_scatter(terms, "author", scatter_dimension=0, tiled=True).astype(jnp.float32)
        z = apply_t(z, author_factor)
        word_factor = whitener(sum_all(gram_of(z)) / words)
        if turn + 1 < ITERS:
            wide = lax.all_gather(z.astype(jnp.bfloat16), "author", axis=0, tiled=True)
            wide, word_factor = lax.optimization_barrier((wide, word_factor))
    author_basis = apply_t(y, author_factor).astype(jnp.bfloat16)
    word_basis = apply_t(z, word_factor).astype(jnp.bfloat16)
    return (author_basis, word_basis)


def solution(mesh):
    return jax.shard_map(
        shards,
        mesh=mesh,
        in_specs=(
            P("author", "word", None, None, None),
            P("author", "word", None),
            P("author", "word", None),
            P("author", "word"),
            P("word", None),
        ),
        out_specs=(P(("author", "word"), None), P(("word", "author"), None)),
        check_vma=False,
    )
```

```python
import functools
import jax
import jax.numpy as jnp
from jax import lax
from jax.experimental import pallas as pl
from jax.experimental.pallas import tpu as pltpu
from jax.sharding import PartitionSpec as P

ITERS = 2
GROUP = 4
AHEAD = 8
BLOCK = 64
HALF = 128
HIGH = lax.Precision.HIGHEST


def product_kernel(
    src_ids, dst_ids, count, values, panel, out, total, part, source, part_sem, source_sem, *, column
):
    size = part.shape[1]
    columns = pl.ds(column, source.shape[2])
    groups = (count[0] + GROUP - 1) // GROUP

    def copies(group):
        first = group * GROUP
        yield pltpu.make_async_copy(
            values.at[pl.ds(first, GROUP)], part.at[pl.ds(first, GROUP)], part_sem.at[group]
        )
        for offset in range(GROUP):
            slot = first + offset
            rows = pl.ds(pl.multiple_of(src_ids[slot] * size, size), size)
            yield pltpu.make_async_copy(panel.at[rows, columns], source.at[slot], source_sem.at[slot])

    def start(group, carry):
        for copy in copies(group):
            copy.start()
        return carry

    def clear(index, carry):
        total[index] = jnp.zeros_like(total[index])
        return carry

    def work(group, carry):
        @pl.when(group + AHEAD < groups)
        def _():
            start(group + AHEAD, 0)

        for copy in copies(group):
            copy.wait()
        first = group * GROUP
        prods = [
            jnp.dot(part[first + offset], source[first + offset], preferred_element_type=jnp.float32)
            for offset in range(GROUP)
        ]
        for offset in range(GROUP):
            total[dst_ids[first + offset]] += prods[offset]
        return carry

    def emit(index, carry):
        out[pl.ds(pl.multiple_of(index * size, size), size), :] = total[index].astype(out.dtype)
        return carry

    lax.fori_loop(0, jnp.minimum(AHEAD, groups), start, 0)
    lax.fori_loop(0, total.shape[0], clear, 0)
    lax.fori_loop(0, groups, work, 0)
    lax.fori_loop(0, out.shape[0] // size, emit, 0)


def product_t_kernel(src_ids, dst_ids, count, values, panel, out, total, part, staged, part_sem, out_sem):
    size = part.shape[1]
    groups = (count[0] + GROUP - 1) // GROUP

    def fetch(group):
        span = pl.ds(group * GROUP, GROUP)
        return pltpu.make_async_copy(values.at[span], part.at[span], part_sem.at[group])

    def start(group, carry):
        fetch(group).start()
        return carry

    def clear(index, carry):
        total[index] = jnp.zeros_like(total[index])
        return carry

    def work(group, carry):
        fetch(group).wait()
        first = group * GROUP
        prods = []
        for offset in range(GROUP):
            rows = pl.ds(pl.multiple_of(src_ids[first + offset] * size, size), size)
            prods.append(
                lax.dot_general(
                    part[first + offset],
                    panel[rows, :],
                    (((0,), (0,)), ((), ())),
                    preferred_element_type=jnp.float32,
                )
            )
        for offset in range(GROUP):
            total[dst_ids[first + offset]] += prods[offset]
        return carry

    def emit(index, carry):
        staged[pl.ds(pl.multiple_of(index * size, size), size), :] = total[index].astype(staged.dtype)
        return carry

    lax.fori_loop(0, groups, start, 0)
    lax.fori_loop(0, total.shape[0], clear, 0)
    lax.fori_loop(0, groups, work, 0)
    blocks = out.shape[0] // size
    pieces = out_sem.shape[0]
    sends = []
    for piece in range(pieces):
        lax.fori_loop(piece * blocks // pieces, (piece + 1) * blocks // pieces, emit, 0)
        rows = pl.ds(piece * out.shape[0] // pieces, out.shape[0] // pieces)
        sends.append(pltpu.make_async_copy(staged.at[rows], out.at[rows], out_sem.at[piece]))
        sends[-1].start()
    for send in sends:
        send.wait()


def product(values, src_ids, dst_ids, count, panel, out_blocks, transpose, column=0):
    cap, size, _ = values.shape
    width = HALF
    dst_ids = jnp.where(jnp.arange(cap, dtype=jnp.int32) < count, dst_ids, out_blocks)
    smem = pl.BlockSpec(memory_space=pltpu.SMEM)
    vmem = pl.BlockSpec(memory_space=pltpu.VMEM)
    whole = pl.BlockSpec(memory_space=pl.ANY)
    values = pltpu.with_memory_space_constraint(values, pltpu.HBM)
    rows = out_blocks * size
    scratch = [
        pltpu.VMEM((out_blocks + 1, size, width), jnp.float32),
        pltpu.VMEM((cap, size, size), values.dtype),
    ]
    if transpose:
        kernel, panel_spec, out_spec = product_t_kernel, vmem, whole
        out_shape = pltpu.HBM((rows, width), jnp.bfloat16)
        scratch += [pltpu.VMEM((rows, width), jnp.bfloat16)]
        scratch += [pltpu.SemaphoreType.DMA((cap // GROUP,)), pltpu.SemaphoreType.DMA((8,))]
    else:
        kernel = functools.partial(product_kernel, column=column)
        panel_spec, out_spec = whole, vmem
        panel = pltpu.with_memory_space_constraint(panel, pltpu.HBM)
        out_shape = pltpu.VMEM((rows, width), jnp.bfloat16)
        scratch += [pltpu.VMEM((cap, size, width), panel.dtype)]
        scratch += [pltpu.SemaphoreType.DMA((cap // GROUP,)), pltpu.SemaphoreType.DMA((cap,))]
    return pl.pallas_call(
        kernel,
        out_shape=out_shape,
        in_specs=[smem, smem, smem, whole, panel_spec],
        out_specs=out_spec,
        scratch_shapes=scratch,
        compiler_params=pltpu.CompilerParams(vmem_limit_bytes=20 * 1024 * 1024),
        cost_estimate=pl.CostEstimate(
            flops=2 * cap * size * size * width,
            bytes_accessed=2 * (cap * size * size + cap * size * width + rows * width),
            transcendentals=0,
        ),
        name="product_t" if transpose else "product",
    )(src_ids, dst_ids, count.reshape(1), values, panel)


def fold_kernel(parts, earlier, factor, raw, field, copies):
    total = parts[0].astype(jnp.float32)
    for index in range(1, parts.shape[0]):
        total += parts[index].astype(jnp.float32)
    raw[...] = total
    if factor is not None:
        if earlier is not None:
            total = jnp.concatenate([earlier[...], total], axis=1)
        total = apply_t(total, factor[...])
    field[...] = total
    short = total.astype(copies.dtype)
    for index in range(copies.shape[0]):
        copies[index] = short


def fold(parts, earlier, factor):
    vmem = pl.BlockSpec(memory_space=pltpu.VMEM)
    given = [earlier is not None, factor is not None]
    operands = [parts] + [array for array in (earlier, factor) if array is not None]

    def kernel(*refs):
        rest = list(refs[1:])
        optional = [rest.pop(0) if there else None for there in given]
        fold_kernel(refs[0], *optional, *rest)

    field = pltpu.VMEM(parts.shape[1:], jnp.float32)
    return pl.pallas_call(
        kernel,
        out_shape=(field, field, pltpu.VMEM(parts.shape, jnp.bfloat16)),
        in_specs=[vmem] * len(operands),
        out_specs=(vmem, vmem, vmem),
        name="fold",
    )(*operands)


def gram_kernel(left, right, out):
    total = jnp.zeros(out.shape, jnp.float32)
    step = 512
    for start in range(0, left.shape[0], step):
        rows = pl.ds(start, step)
        field = jnp.concatenate([left[rows, :], right[rows, :]], axis=1)
        total += lax.dot_general(
            field, field, (((0,), (0,)), ((), ())), preferred_element_type=jnp.float32
        )
    out[...] = total


def gram_short(left, right):
    vmem = pl.BlockSpec(memory_space=pltpu.VMEM)
    width = left.shape[1] + right.shape[1]
    return pl.pallas_call(
        gram_kernel,
        out_shape=jax.ShapeDtypeStruct((width, width), jnp.float32),
        in_specs=[vmem, vmem],
        out_specs=vmem,
        name="gram_short",
    )(left, right)


def gram_of(field):
    return lax.dot_general(
        field, field, (((0,), (0,)), ((), ())), precision=HIGH, preferred_element_type=jnp.float32
    )


def hop_core(array):
    return lax.ppermute(array, "author", [(i, i ^ 1) for i in range(8)])


def hop_x(array, k):
    return lax.ppermute(array, "author", [(i, (i + 2 * k) % 8) for i in range(8)])


def hop_y(array, k):
    return lax.ppermute(array, "word", [(i, (i + 4 * k) % 16) for i in range(16)])


def hop_z(array, k):
    return lax.ppermute(array, "word", [(i, (i // 4) * 4 + (i + k) % 4) for i in range(16)])


def pick(array, index):
    return lax.dynamic_index_in_dim(array, index, 0, keepdims=False)


def split_core(gram, core):
    halves = gram.reshape(2, gram.shape[0] // 2, gram.shape[1])
    return pick(halves, core) + hop_core(pick(halves, 1 - core))


def join_core(half, core):
    other = hop_core(half)
    return jnp.where(core == 0, jnp.concatenate([half, other]), jnp.concatenate([other, half]))


def sum_author(gram):
    core = lax.axis_index("author") % 2
    half = split_core(gram, core)
    parts = [hop_x(half, k) for k in (1, 3, 2)]
    half = (half + parts[2]) + (parts[0] + parts[1])
    return join_core(half, core)


def sum_all(gram):
    place = lax.axis_index("author")
    core, x = place % 2, place // 2
    half = split_core(gram, core)
    chunks = half.reshape(4, half.shape[0] // 4, half.shape[1])
    got = [hop_x(pick(chunks, (x + k) % 4), k) for k in (1, 3, 2)]
    part = (pick(chunks, x) + got[2]) + (got[0] + got[1])
    for hop in (hop_y, hop_z):
        got = [hop(part, k) for k in (1, 3, 2)]
        part = (part + got[2]) + (got[0] + got[1])
    ring = jnp.stack([part] + [hop_x(part, k) for k in (1, 2, 3)])
    half = jnp.take(ring, (x - jnp.arange(4)) % 4, axis=0).reshape(half.shape)
    return join_core(half, core)


def eliminate(strips):
    shape = strips[0].shape
    sub = lax.broadcasted_iota(jnp.int32, shape, 0)
    half = shape[1] // 2

    def column(strip, lane):
        return jnp.broadcast_to(strip[:, lane : lane + 1], shape)

    def row(strip, j):
        return jnp.broadcast_to(strip[j : j + 1, :], shape)

    for p in range(len(strips)):
        lead = strips[p]
        lanes = [half + 8 * p + j for j in range(8)]
        cols = [column(lead, lane) for lane in lanes]
        below = {i: [column(strips[i], lane) for lane in lanes] for i in range(p + 1, len(strips))}
        scale = jnp.zeros(shape, jnp.float32)
        for j in range(0, 8, 2):
            a, b, c = row(cols[j], j), row(cols[j + 1], j), row(cols[j + 1], j + 1)
            inv0 = 1.0 / a
            inv1 = a / (a * c - b * b)
            m0 = jnp.where(sub > j, cols[j] * inv0, 0.0)
            m1 = jnp.where(sub > j + 1, (cols[j + 1] - m0 * b) * inv1, 0.0)
            top0 = row(lead, j)
            top1 = row(lead, j + 1) - (b * inv0) * top0
            lead = (lead - m0 * top0) - m1 * top1
            scale = jnp.where(sub == j, lax.rsqrt(a), scale)
            scale = jnp.where(sub == j + 1, jnp.sqrt(inv1), scale)
            tops = []
            for k in range(j + 2, 8):
                u0 = row(cols[k], j)
                u1 = row(cols[k], j + 1) - (b * inv0) * u0
                cols[k] = (cols[k] - m0 * u0) - m1 * u1
                tops.append((u0, u1))
            for i, col in below.items():
                n0 = col[j] * inv0
                n1 = (col[j + 1] - n0 * b) * inv1
                for k, (u0, u1) in zip(range(j + 2, 8), tops):
                    col[k] = (col[k] - n0 * u0) - n1 * u1
                strips[i] = (strips[i] - n0 * top0) - n1 * top1
        strips[p] = lead * scale
    return strips


def whiten_kernel(g_ref, out_ref, s_ref, y_ref):
    n = g_ref.shape[0]
    g = g_ref[...]
    eye = lax.broadcasted_iota(jnp.int32, (n, n), 0) == lax.broadcasted_iota(jnp.int32, (n, n), 1)
    diag = jnp.where(eye, g, 0.0)
    across = lax.rsqrt(jnp.sum(diag, axis=0, keepdims=True))
    down = lax.rsqrt(jnp.sum(diag, axis=1, keepdims=True))
    s_ref[...] = g * across * down
    y_ref[...] = jnp.where(eye, 1.0, 0.0)
    lane = lax.broadcasted_iota(jnp.int32, (BLOCK, n), 1)
    def stage(at, carry):
        rows = pl.ds(pl.multiple_of(at * BLOCK, BLOCK), BLOCK)
        left, right = s_ref[rows, :], y_ref[rows, :]
        turned = pltpu.roll(left, lax.rem(n + BLOCK - at * BLOCK, n), 1)[:, : 2 * BLOCK]
        i0 = lax.broadcasted_iota(jnp.int32, turned.shape, 0)
        i1 = lax.broadcasted_iota(jnp.int32, turned.shape, 1)
        start = jnp.where(i1 < BLOCK, jnp.where(i0 == i1, 1.0, 0.0), turned)
        strips = eliminate([start[8 * i : 8 * i + 8] for i in range(BLOCK // 8)])
        inverse = jnp.concatenate(strips, axis=0)[:, :BLOCK]
        dot = lambda u, v, d: lax.dot_general(u, v, (((d,), (0,)), ((), ())), precision=HIGH, preferred_element_type=jnp.float32)
        left = dot(inverse, left, 1)
        right = dot(inverse, right, 1)
        rest = jnp.where(lane >= (at + 1) * BLOCK, left, 0.0)
        s_ref[...] -= dot(rest, left, 0)
        y_ref[...] -= dot(rest, right, 0)
        y_ref[rows, :] = right
        return carry
    lax.fori_loop(0, n // BLOCK, stage, 0)
    out_ref[...] = y_ref[...] * across


def whitener(gram):
    return pl.pallas_call(
        whiten_kernel,
        out_shape=jax.ShapeDtypeStruct(gram.shape, jnp.float32),
        scratch_shapes=[pltpu.VMEM(gram.shape, jnp.float32)] * 2,
        cost_estimate=pl.CostEstimate(flops=10**9, bytes_accessed=40 * 10**6, transcendentals=0),
        name="whitener",
    )(gram)


def apply_t(field, inverse):
    return lax.dot_general(
        field, inverse, (((1,), (1,)), ((), ())), precision=HIGH, preferred_element_type=jnp.float32
    )


def swap_word(parts):
    return lax.all_to_all(parts, "word", 0, 0)


def rows_of(factor, half):
    if factor is None:
        return None
    return factor[half * HALF : (half + 1) * HALF, : (half + 1) * HALF]


def apply_half(raws, factor, half):
    field = jnp.concatenate(raws[: half + 1], axis=1)
    return apply_t(field, rows_of(factor, half))


def shards(block_values, block_rows, block_cols, block_count, omega):
    values = block_values[0, 0]
    rows = block_rows[0, 0]
    cols = block_cols[0, 0]
    count = block_count[0, 0]
    size = values.shape[1]
    word_blocks = omega.shape[0] // size
    author_blocks = 32
    authors = author_blocks * size * lax.axis_size("author")
    words = word_blocks * size * lax.axis_size("word")
    halves = range(omega.shape[1] // HALF)
    wide = [omega for half in halves]
    word_factor = None
    for turn in range(ITERS):
        y, y_raw, y_rows, z_raw = [], [], [], []
        for half in halves:
            column = half * HALF if turn == 0 else 0
            terms = product(values, cols, rows, count, wide[half], author_blocks, False, column)
            raw, field, copies = fold(
                swap_word(terms.reshape(16, -1, HALF)),
                y_raw[0] if half and word_factor is not None else None,
                rows_of(word_factor, half),
            )
            y_raw.append(raw)
            y.append(field)
            y_rows.append(swap_word(copies).reshape(terms.shape))
            terms = product(values, rows, cols, count, y_rows[half], word_blocks, True)
            share = lax.psum_scatter(terms, "author", scatter_dimension=0, tiled=True)
            z_raw.append(share.astype(jnp.float32))
        author_factor = whitener(sum_author(gram_short(*y_rows)) / authors)
        z = [apply_half(z_raw, author_factor, half) for half in halves]
        gram = sum_all(gram_of(jnp.concatenate(z, axis=1))) / words
        if turn + 1 < ITERS:
            wide = [lax.all_gather(part.astype(jnp.bfloat16), "author", axis=0, tiled=True) for part in z]
            wide[0], gram = lax.optimization_barrier((wide[0], gram))
        word_factor = whitener(gram)
    author_basis = apply_t(jnp.concatenate(y, axis=1), author_factor).astype(jnp.bfloat16)
    word_basis = apply_t(jnp.concatenate(z, axis=1), word_factor).astype(jnp.bfloat16)
    return (author_basis, word_basis)


def solution(mesh):
    return jax.shard_map(
        shards,
        mesh=mesh,
        in_specs=(
            P("author", "word", None, None, None),
            P("author", "word", None),
            P("author", "word", None),
            P("author", "word"),
            P("word", None),
        ),
        out_specs=(P(("author", "word"), None), P(("word", "author"), None)),
        check_vma=False,
    )
```

```python
import jax
import jax.numpy as jnp
from jax import lax
from jax.experimental import pallas as pl
from jax.experimental.pallas import tpu as pltpu
from jax.sharding import PartitionSpec as P

ITERS = 2
GROUP = 16
CUT = 2048
PLACE = 1024
BLOCK = 64
HIGH = lax.Precision.HIGHEST


def product_kernel(src_ids, dst_ids, count, places, values, *refs):
    pieces, (out, total, part, panel, part_sem, piece_sem) = refs[:-6], refs[-6:]
    size = part.shape[1]
    groups = (count[0] + GROUP - 1) // GROUP

    def fetch(group):
        span = pl.ds(group * GROUP, GROUP)
        return pltpu.make_async_copy(values.at[span], part.at[span], part_sem.at[group])

    def start(group, carry):
        fetch(group).start()
        return carry

    def clear(index, carry):
        total[index] = jnp.zeros_like(total[index])
        return carry

    def work(group, carry):
        fetch(group).wait()
        first = group * GROUP
        prods = []
        for offset in range(GROUP):
            rows = pl.ds(pl.multiple_of(src_ids[first + offset] * size, size), size)
            prods.append(jnp.dot(part[first + offset], panel[rows, :], preferred_element_type=jnp.float32))
        for offset in range(GROUP):
            total[dst_ids[first + offset]] += prods[offset]
        return carry

    def emit(index, carry):
        out[pl.ds(pl.multiple_of(index * size, size), size), :] = total[index].astype(out.dtype)
        return carry

    moves = []
    for index, piece in enumerate(pieces):
        length = min(CUT, piece.shape[0])
        for at in range(0, piece.shape[0], length):
            target = pl.ds(pl.multiple_of(places[index] * PLACE + at, PLACE), length)
            moves.append((piece.at[pl.ds(at, length)], panel.at[target]))
    moves = [pltpu.make_async_copy(*move, piece_sem.at[index]) for index, move in enumerate(moves)]
    fetch(0).start()
    for move in moves:
        move.start()
    lax.fori_loop(1, groups, start, 0)
    lax.fori_loop(0, total.shape[0], clear, 0)
    for move in moves:
        move.wait()
    lax.fori_loop(0, groups, work, 0)
    lax.fori_loop(0, out.shape[0] // size, emit, 0)


def product_t_kernel(src_ids, dst_ids, count, core, values, panel, out, total, part, slots, part_sem):
    size = part.shape[1]
    share = out.shape[0] // size // 4
    spare = total.shape[0] - 1
    groups = (count[0] + GROUP - 1) // GROUP

    def fetch(group):
        span = pl.ds(group * GROUP, GROUP)
        return pltpu.make_async_copy(values.at[span], part.at[span], part_sem.at[group])

    def start(group, carry):
        fetch(group).start()
        return carry

    def wait(group, carry):
        fetch(group).wait()
        return carry

    def clear(index, carry):
        total[index] = jnp.zeros_like(total[index])
        return carry

    def choose(slot, chosen):
        slots[chosen] = slot
        return chosen + jnp.where((dst_ids[slot] // share) % 2 == core[0], 1, 0)

    lax.fori_loop(0, groups, start, 0)
    lax.fori_loop(0, total.shape[0], clear, 0)
    chosen = lax.fori_loop(0, count[0], choose, 0)
    for offset in range(GROUP):
        slots[chosen + offset] = 0
    lax.fori_loop(0, groups, wait, 0)

    def work(group, carry):
        prods, targets = [], []
        for offset in range(GROUP):
            index = group * GROUP + offset
            slot = slots[index]
            place = dst_ids[slot]
            place = (place // (2 * share)) * share + place % share
            targets.append(jnp.where(index < chosen, place, spare))
            rows = pl.ds(pl.multiple_of(src_ids[slot] * size, size), size)
            prods.append(
                lax.dot_general(
                    part[slot], panel[rows, :], (((0,), (0,)), ((), ())), preferred_element_type=jnp.float32
                )
            )
        for target, prod in zip(targets, prods):
            total[target] += prod
        return carry

    def emit(index, carry):
        out[pl.ds(pl.multiple_of(index * size, size), size), :] = total[index].astype(out.dtype)
        return carry

    lax.fori_loop(0, (chosen + GROUP - 1) // GROUP, work, 0)
    lax.fori_loop(0, spare, emit, 0)


def kernel_call(kernel, name, operands, specs, rows, width, cap, size, scratch):
    vmem = pl.BlockSpec(memory_space=pltpu.VMEM)
    return pl.pallas_call(
        kernel,
        out_shape=pltpu.VMEM((rows, width), jnp.bfloat16),
        in_specs=specs,
        out_specs=vmem,
        scratch_shapes=[
            pltpu.VMEM((rows // size + 1, size, width), jnp.float32),
            pltpu.VMEM((cap, size, size), jnp.bfloat16),
            *scratch,
        ],
        compiler_params=pltpu.CompilerParams(vmem_limit_bytes=24 * 1024 * 1024),
        cost_estimate=pl.CostEstimate(
            flops=4 * cap * size * size * width, bytes_accessed=20 * 1024 * 1024, transcendentals=0
        ),
        name=name,
    )(*operands)


def product(values, cols, rows, count, pieces, places, out_blocks):
    cap, size, _ = values.shape
    width = pieces[0].shape[1]
    rows = jnp.where(jnp.arange(cap, dtype=jnp.int32) < count, rows, out_blocks)
    smem = pl.BlockSpec(memory_space=pltpu.SMEM)
    whole = pl.BlockSpec(memory_space=pl.ANY)
    values = pltpu.with_memory_space_constraint(values, pltpu.HBM)
    if len(pieces) == 1:
        pieces = [pltpu.with_memory_space_constraint(pieces[0], pltpu.HBM)]
    moves = sum(max(1, piece.shape[0] // CUT) for piece in pieces)
    scratch = [
        pltpu.VMEM((sum(piece.shape[0] for piece in pieces), width), jnp.bfloat16),
        pltpu.SemaphoreType.DMA((cap // GROUP,)),
        pltpu.SemaphoreType.DMA((moves,)),
    ]
    operands = (cols, rows, count.reshape(1), places, values, *pieces)
    specs = [smem] * 4 + [whole] * (1 + len(pieces))
    return kernel_call(
        product_kernel, "product", operands, specs, out_blocks * size, width, cap, size, scratch
    )


def product_t(values, rows, cols, count, panel, word_blocks, core):
    cap, size, _ = values.shape
    width = panel.shape[1]
    smem = pl.BlockSpec(memory_space=pltpu.SMEM)
    whole = pl.BlockSpec(memory_space=pl.ANY)
    vmem = pl.BlockSpec(memory_space=pltpu.VMEM)
    values = pltpu.with_memory_space_constraint(values, pltpu.HBM)
    scratch = [pltpu.SMEM((cap + GROUP,), jnp.int32), pltpu.SemaphoreType.DMA((cap // GROUP,))]
    operands = (rows, cols, count.reshape(1), core.reshape(1), values, panel)
    specs = [smem] * 4 + [whole, vmem]
    half = word_blocks * size // 2
    out = kernel_call(product_t_kernel, "product_t", operands, specs, half, width, cap, size, scratch)
    return out.reshape(4, half // 4, width)


def fold_kernel(parts, factor, field, copies):
    total = parts[0].astype(jnp.float32)
    for index in range(1, parts.shape[0]):
        total += parts[index].astype(jnp.float32)
    if factor is not None:
        total = apply_t(total, factor[...])
    field[...] = total
    short = total.astype(copies.dtype)
    for index in range(copies.shape[0]):
        copies[index] = short


def fold(parts, factor):
    vmem = pl.BlockSpec(memory_space=pltpu.VMEM)
    operands = (parts,) if factor is None else (parts, factor)
    kernel = fold_kernel if factor is not None else lambda p, f, c: fold_kernel(p, None, f, c)
    return pl.pallas_call(
        kernel,
        out_shape=(
            pltpu.VMEM(parts.shape[1:], jnp.float32),
            pltpu.VMEM(parts.shape, jnp.bfloat16),
        ),
        in_specs=[vmem] * len(operands),
        out_specs=(vmem, vmem),
        name="fold",
    )(*operands)


def gram_of(field):
    return lax.dot_general(
        field, field, (((0,), (0,)), ((), ())), precision=HIGH, preferred_element_type=jnp.float32
    )


def hop_core(array):
    return lax.ppermute(array, "author", [(i, i ^ 1) for i in range(8)])


def hop_x(array, k):
    return lax.ppermute(array, "author", [(i, (i + 2 * k) % 8) for i in range(8)])


def hop_y(array, k):
    return lax.ppermute(array, "word", [(i, (i + 4 * k) % 16) for i in range(16)])


def hop_z(array, k):
    return lax.ppermute(array, "word", [(i, (i // 4) * 4 + (i + k) % 4) for i in range(16)])


def pick(array, index):
    return lax.dynamic_index_in_dim(array, index, 0, keepdims=False)


def split_core(gram, core):
    halves = gram.reshape(2, gram.shape[0] // 2, gram.shape[1])
    return pick(halves, core) + hop_core(pick(halves, 1 - core))


def join_core(half, core):
    other = hop_core(half)
    return jnp.where(core == 0, jnp.concatenate([half, other]), jnp.concatenate([other, half]))


def sum_author(gram):
    core = lax.axis_index("author") % 2
    half = split_core(gram, core)
    parts = [hop_x(half, k) for k in (1, 3, 2)]
    half = (half + parts[2]) + (parts[0] + parts[1])
    return join_core(half, core)


def sum_all(gram):
    place = lax.axis_index("author")
    core, x = place % 2, place // 2
    half = split_core(gram, core)
    chunks = half.reshape(4, half.shape[0] // 4, half.shape[1])
    got = [hop_x(pick(chunks, (x + k) % 4), k) for k in (1, 3, 2)]
    part = (pick(chunks, x) + got[2]) + (got[0] + got[1])
    for hop in (hop_y, hop_z):
        got = [hop(part, k) for k in (1, 3, 2)]
        part = (part + got[2]) + (got[0] + got[1])
    ring = jnp.stack([part] + [hop_x(part, k) for k in (1, 2, 3)])
    half = jnp.take(ring, (x - jnp.arange(4)) % 4, axis=0).reshape(half.shape)
    return join_core(half, core)


def eliminate(strips):
    shape = strips[0].shape
    sub = lax.broadcasted_iota(jnp.int32, shape, 0)
    half = shape[1] // 2

    def column(strip, lane):
        return jnp.broadcast_to(strip[:, lane : lane + 1], shape)

    def row(strip, j):
        return jnp.broadcast_to(strip[j : j + 1, :], shape)

    for p in range(len(strips)):
        lead = strips[p]
        lanes = [half + 8 * p + j for j in range(8)]
        cols = [column(lead, lane) for lane in lanes]
        below = {i: [column(strips[i], lane) for lane in lanes] for i in range(p + 1, len(strips))}
        scale = jnp.zeros(shape, jnp.float32)
        for j in range(0, 8, 2):
            a, b, c = row(cols[j], j), row(cols[j + 1], j), row(cols[j + 1], j + 1)
            inv0 = 1.0 / a
            inv1 = a / (a * c - b * b)
            m0 = jnp.where(sub > j, cols[j] * inv0, 0.0)
            m1 = jnp.where(sub > j + 1, (cols[j + 1] - m0 * b) * inv1, 0.0)
            top0 = row(lead, j)
            top1 = row(lead, j + 1) - (b * inv0) * top0
            lead = (lead - m0 * top0) - m1 * top1
            scale = jnp.where(sub == j, lax.rsqrt(a), scale)
            scale = jnp.where(sub == j + 1, jnp.sqrt(inv1), scale)
            tops = []
            for k in range(j + 2, 8):
                u0 = row(cols[k], j)
                u1 = row(cols[k], j + 1) - (b * inv0) * u0
                cols[k] = (cols[k] - m0 * u0) - m1 * u1
                tops.append((u0, u1))
            for i, col in below.items():
                n0 = col[j] * inv0
                n1 = (col[j + 1] - n0 * b) * inv1
                for k, (u0, u1) in zip(range(j + 2, 8), tops):
                    col[k] = (col[k] - n0 * u0) - n1 * u1
                strips[i] = (strips[i] - n0 * top0) - n1 * top1
        strips[p] = lead * scale
    return strips


def whiten_kernel(g_ref, out_ref, s_ref, y_ref):
    n = g_ref.shape[0]
    g = g_ref[...]
    eye = lax.broadcasted_iota(jnp.int32, (n, n), 0) == lax.broadcasted_iota(jnp.int32, (n, n), 1)
    diag = jnp.where(eye, g, 0.0)
    across = lax.rsqrt(jnp.sum(diag, axis=0, keepdims=True))
    down = lax.rsqrt(jnp.sum(diag, axis=1, keepdims=True))
    s_ref[...] = g * across * down
    y_ref[...] = jnp.where(eye, 1.0, 0.0)
    lane = lax.broadcasted_iota(jnp.int32, (BLOCK, n), 1)
    def stage(at, carry):
        rows = pl.ds(pl.multiple_of(at * BLOCK, BLOCK), BLOCK)
        left, right = s_ref[rows, :], y_ref[rows, :]
        turned = pltpu.roll(left, lax.rem(n + BLOCK - at * BLOCK, n), 1)[:, : 2 * BLOCK]
        i0 = lax.broadcasted_iota(jnp.int32, turned.shape, 0)
        i1 = lax.broadcasted_iota(jnp.int32, turned.shape, 1)
        start = jnp.where(i1 < BLOCK, jnp.where(i0 == i1, 1.0, 0.0), turned)
        strips = eliminate([start[8 * i : 8 * i + 8] for i in range(BLOCK // 8)])
        inverse = jnp.concatenate(strips, axis=0)[:, :BLOCK]
        dot = lambda u, v, d: lax.dot_general(u, v, (((d,), (0,)), ((), ())), precision=HIGH, preferred_element_type=jnp.float32)
        left = dot(inverse, left, 1)
        right = dot(inverse, right, 1)
        rest = jnp.where(lane >= (at + 1) * BLOCK, left, 0.0)
        s_ref[...] -= dot(rest, left, 0)
        y_ref[...] -= dot(rest, right, 0)
        y_ref[rows, :] = right
        return carry
    lax.fori_loop(0, n // BLOCK, stage, 0)
    out_ref[...] = y_ref[...] * across


def whitener(gram):
    return pl.pallas_call(
        whiten_kernel,
        out_shape=jax.ShapeDtypeStruct(gram.shape, jnp.float32),
        scratch_shapes=[pltpu.VMEM(gram.shape, jnp.float32)] * 2,
        cost_estimate=pl.CostEstimate(flops=10**9, bytes_accessed=40 * 10**6, transcendentals=0),
        name="whitener",
    )(gram)


def apply_t(field, inverse):
    return lax.dot_general(
        field, inverse, (((1,), (1,)), ((), ())), precision=HIGH, preferred_element_type=jnp.float32
    )


def swap_word(parts):
    return lax.all_to_all(parts, "word", 0, 0)


def short(array):
    return array.astype(jnp.bfloat16)


def long(array):
    return array.astype(jnp.float32)


def scatter_author(values, rows, cols, count, y_rows, word_blocks):
    place = lax.axis_index("author")
    core, x = place % 2, place // 2
    theirs = product_t(values, rows, cols, count, y_rows, word_blocks, 1 - core)
    mine = product_t(values, rows, cols, count, y_rows, word_blocks, core)
    got = hop_core(theirs)

    def chunk(k):
        index = (x + k) % 4
        return long(pick(mine, index)) + long(pick(got, index))

    mid = mine.shape[1] // 2
    far = short(chunk(2))
    first, last = hop_x(far[:mid], 1), hop_x(far[mid:], 3)
    up, down = chunk(1), chunk(3)
    up_last, down_first = hop_x(short(up[mid:]), 1), hop_x(short(down[:mid]), 3)
    up_first = hop_x(short(up[:mid] + long(first)), 1)
    down_last = hop_x(short(down[mid:] + long(last)), 3)
    here = chunk(0)
    return jnp.concatenate(
        [
            here[:mid] + long(up_first) + long(down_first),
            here[mid:] + long(up_last) + long(down_last),
        ]
    )


def gather_author(share):
    place = lax.axis_index("author")
    core, x = place % 2, place // 2
    mid = share.shape[0] // 2
    above, below = hop_x(share, 1), hop_x(share, 3)
    pieces = [share, above, below, hop_x(above[:mid], 1), hop_x(below[mid:], 3)]
    pieces += [hop_core(piece) for piece in pieces]
    chips = jnp.stack([x, (x + 3) % 4, (x + 1) % 4, (x + 2) % 4, (x + 2) % 4])
    extra = jnp.array([0, 0, 0, 0, 1], jnp.int32)
    width = share.shape[0] // PLACE
    places = [(chips * 2 + c) * width + extra for c in (core, 1 - core)]
    return pieces, jnp.concatenate(places).astype(jnp.int32)


def shards(block_values, block_rows, block_cols, block_count, omega):
    values = block_values[0, 0]
    rows = block_rows[0, 0]
    cols = block_cols[0, 0]
    count = block_count[0, 0]
    size = values.shape[1]
    word_blocks = omega.shape[0] // size
    author_blocks = 32
    authors = author_blocks * size * lax.axis_size("author")
    words = word_blocks * size * lax.axis_size("word")
    pieces, places = [omega], jnp.zeros((1,), jnp.int32)
    word_factor = None
    for turn in range(ITERS):
        terms = product(values, cols, rows, count, pieces, places, author_blocks)
        y, copies = fold(swap_word(terms.reshape(16, -1, terms.shape[1])), word_factor)
        y_rows = swap_word(copies).reshape(terms.shape)
        z = scatter_author(values, rows, cols, count, y_rows, word_blocks)
        author_factor = whitener(
            sum_author(lax.dot_general(y_rows, y_rows, (((0,), (0,)), ((), ())), preferred_element_type=jnp.float32))
            / authors
        )
        z = apply_t(z, author_factor)
        if turn + 1 < ITERS:
            pieces, places = gather_author(short(z))
        word_factor = whitener(sum_all(gram_of(z)) / words)
        if turn + 1 < ITERS:
            pieces, word_factor = lax.optimization_barrier((pieces, word_factor))
    author_basis = short(apply_t(y, author_factor))
    word_basis = short(apply_t(z, word_factor))
    return (author_basis, word_basis)


def solution(mesh):
    return jax.shard_map(
        shards,
        mesh=mesh,
        in_specs=(
            P("author", "word", None, None, None),
            P("author", "word", None),
            P("author", "word", None),
            P("author", "word"),
            P("word", None),
        ),
        out_specs=(P(("author", "word"), None), P(("word", "author"), None)),
        check_vma=False,
    )
```

```python
import jax
import jax.numpy as jnp
from jax import lax
from jax.experimental import pallas as pl
from jax.experimental.pallas import tpu as pltpu
from jax.sharding import PartitionSpec as P

ITERS = 2
GROUP = 16
CUT = 2048
BLOCK = 64
HIGH = lax.Precision.HIGHEST
MIDDLE = lax.Precision.HIGH


def product_kernel(src_ids, dst_ids, count, values, given, out, total, part, panel, part_sem, panel_sem):
    size = part.shape[1]
    groups = (count[0] + GROUP - 1) // GROUP

    def fetch(group):
        span = pl.ds(group * GROUP, GROUP)
        return pltpu.make_async_copy(values.at[span], part.at[span], part_sem.at[group])

    def start(group, carry):
        fetch(group).start()
        return carry

    def clear(index, carry):
        total[index] = jnp.zeros_like(total[index])
        return carry

    def work(group, carry):
        fetch(group).wait()
        first = group * GROUP
        prods = []
        for offset in range(GROUP):
            rows = pl.ds(pl.multiple_of(src_ids[first + offset] * size, size), size)
            prods.append(jnp.dot(part[first + offset], panel[rows, :], preferred_element_type=jnp.float32))
        for offset in range(GROUP):
            total[dst_ids[first + offset]] += prods[offset]
        return carry

    def emit(index, carry):
        out[pl.ds(pl.multiple_of(index * size, size), size), :] = total[index].astype(out.dtype)
        return carry

    moves = []
    for index in range(panel_sem.shape[0]):
        rows = pl.ds(index * CUT, CUT)
        moves.append(pltpu.make_async_copy(given.at[rows], panel.at[rows], panel_sem.at[index]))
    fetch(0).start()
    for move in moves:
        move.start()
    lax.fori_loop(1, groups, start, 0)
    lax.fori_loop(0, total.shape[0], clear, 0)
    for move in moves:
        move.wait()
    lax.fori_loop(0, groups, work, 0)
    lax.fori_loop(0, out.shape[0] // size, emit, 0)


def product_t_kernel(src_ids, dst_ids, count, values, panel, out, total, part, staged, part_sem, out_sem):
    size = part.shape[1]
    groups = (count[0] + GROUP - 1) // GROUP

    def fetch(group):
        span = pl.ds(group * GROUP, GROUP)
        return pltpu.make_async_copy(values.at[span], part.at[span], part_sem.at[group])

    def start(group, carry):
        fetch(group).start()
        return carry

    def clear(index, carry):
        total[index] = jnp.zeros_like(total[index])
        return carry

    def work(group, carry):
        fetch(group).wait()
        first = group * GROUP
        prods = []
        for offset in range(GROUP):
            rows = pl.ds(pl.multiple_of(src_ids[first + offset] * size, size), size)
            prods.append(
                lax.dot_general(
                    part[first + offset],
                    panel[rows, :],
                    (((0,), (0,)), ((), ())),
                    preferred_element_type=jnp.float32,
                )
            )
        for offset in range(GROUP):
            total[dst_ids[first + offset]] += prods[offset]
        return carry

    def emit(index, carry):
        staged[pl.ds(pl.multiple_of(index * size, size), size), :] = total[index].astype(staged.dtype)
        return carry

    lax.fori_loop(0, groups, start, 0)
    lax.fori_loop(0, total.shape[0], clear, 0)
    lax.fori_loop(0, groups, work, 0)
    blocks = out.shape[0] // size
    pieces = out_sem.shape[0]
    sends = []
    for piece in range(pieces):
        lax.fori_loop(piece * blocks // pieces, (piece + 1) * blocks // pieces, emit, 0)
        rows = pl.ds(piece * out.shape[0] // pieces, out.shape[0] // pieces)
        sends.append(pltpu.make_async_copy(staged.at[rows], out.at[rows], out_sem.at[piece]))
        sends[-1].start()
    for send in sends:
        send.wait()


def kernel_call(kernel, name, operands, specs, out, cap, size, scratch):
    rows, width = out.shape
    return pl.pallas_call(
        kernel,
        out_shape=out,
        in_specs=specs,
        out_specs=pl.BlockSpec(memory_space=pltpu.VMEM if name == "product" else pl.ANY),
        scratch_shapes=[
            pltpu.VMEM((rows // size + 1, size, width), jnp.float32),
            pltpu.VMEM((cap, size, size), jnp.bfloat16),
            *scratch,
        ],
        compiler_params=pltpu.CompilerParams(vmem_limit_bytes=36 * 1024 * 1024),
        cost_estimate=pl.CostEstimate(
            flops=4 * cap * size * size * width, bytes_accessed=20 * 1024 * 1024, transcendentals=0
        ),
        name=name,
    )(*operands)


def product(values, cols, rows, count, panel, out_blocks):
    cap, size, _ = values.shape
    width = panel.shape[1]
    rows = jnp.where(jnp.arange(cap, dtype=jnp.int32) < count, rows, out_blocks)
    smem = pl.BlockSpec(memory_space=pltpu.SMEM)
    whole = pl.BlockSpec(memory_space=pl.ANY)
    values = pltpu.with_memory_space_constraint(values, pltpu.HBM)
    panel = pltpu.with_memory_space_constraint(panel, pltpu.HBM)
    scratch = [
        pltpu.VMEM(panel.shape, jnp.bfloat16),
        pltpu.SemaphoreType.DMA((cap // GROUP,)),
        pltpu.SemaphoreType.DMA((panel.shape[0] // CUT,)),
    ]
    operands = (cols, rows, count.reshape(1), values, panel)
    specs = [smem] * 3 + [whole] * 2
    out = pltpu.VMEM((out_blocks * size, width), jnp.bfloat16)
    return kernel_call(product_kernel, "product", operands, specs, out, cap, size, scratch)


def product_t(values, rows, cols, count, panel, out_blocks):
    cap, size, _ = values.shape
    cols = jnp.where(jnp.arange(cap, dtype=jnp.int32) < count, cols, out_blocks)
    smem = pl.BlockSpec(memory_space=pltpu.SMEM)
    whole = pl.BlockSpec(memory_space=pl.ANY)
    vmem = pl.BlockSpec(memory_space=pltpu.VMEM)
    values = pltpu.with_memory_space_constraint(values, pltpu.HBM)
    out = pltpu.HBM((out_blocks * size, panel.shape[1]), jnp.bfloat16)
    scratch = [
        pltpu.VMEM(out.shape, jnp.bfloat16),
        pltpu.SemaphoreType.DMA((cap // GROUP,)),
        pltpu.SemaphoreType.DMA((8,)),
    ]
    operands = (rows, cols, count.reshape(1), values, panel)
    specs = [smem] * 3 + [whole, vmem]
    return kernel_call(product_t_kernel, "product_t", operands, specs, out, cap, size, scratch)


def fold_kernel(parts, factor, field, copies):
    total = parts[0].astype(jnp.float32)
    for index in range(1, parts.shape[0]):
        total += parts[index].astype(jnp.float32)
    if factor is not None:
        total = apply_t(total, factor[...], HIGH)
    field[...] = total
    short = total.astype(copies.dtype)
    for index in range(copies.shape[0]):
        copies[index] = short


def fold(parts, factor):
    vmem = pl.BlockSpec(memory_space=pltpu.VMEM)
    operands = (parts,) if factor is None else (parts, factor)
    kernel = fold_kernel if factor is not None else lambda p, f, c: fold_kernel(p, None, f, c)
    return pl.pallas_call(
        kernel,
        out_shape=(
            pltpu.VMEM(parts.shape[1:], jnp.float32),
            pltpu.VMEM(parts.shape, jnp.bfloat16),
        ),
        in_specs=[vmem] * len(operands),
        out_specs=(vmem, vmem),
        name="fold",
    )(*operands)


def gram_kernel(field, out):
    total = jnp.zeros(out.shape, jnp.float32)
    step = 512
    for start in range(0, field.shape[0], step):
        part = field[pl.ds(start, step), :]
        total += lax.dot_general(part, part, (((0,), (0,)), ((), ())), preferred_element_type=jnp.float32)
    out[...] = total


def gram_short(field):
    vmem = pl.BlockSpec(memory_space=pltpu.VMEM)
    return pl.pallas_call(
        gram_kernel,
        out_shape=jax.ShapeDtypeStruct((field.shape[1],) * 2, jnp.float32),
        in_specs=[vmem],
        out_specs=vmem,
        name="gram_short",
    )(field)


def gram_of(field):
    return lax.dot_general(
        field, field, (((0,), (0,)), ((), ())), precision=MIDDLE, preferred_element_type=jnp.float32
    )


def hop_core(array):
    return lax.ppermute(array, "author", [(i, i ^ 1) for i in range(8)])


def hop_x(array, k):
    return lax.ppermute(array, "author", [(i, (i + 2 * k) % 8) for i in range(8)])


def hop_y(array, k):
    return lax.ppermute(array, "word", [(i, (i + 4 * k) % 16) for i in range(16)])


def hop_z(array, k):
    return lax.ppermute(array, "word", [(i, (i // 4) * 4 + (i + k) % 4) for i in range(16)])


def pick(array, index):
    return lax.dynamic_index_in_dim(array, index, 0, keepdims=False)


def split_core(gram, core):
    halves = gram.reshape(2, gram.shape[0] // 2, gram.shape[1])
    return pick(halves, core) + hop_core(pick(halves, 1 - core))


def join_core(half, core):
    other = hop_core(half)
    return jnp.where(core == 0, jnp.concatenate([half, other]), jnp.concatenate([other, half]))


def sum_author(gram):
    core = lax.axis_index("author") % 2
    half = split_core(gram, core)
    parts = [hop_x(half, k) for k in (1, 3, 2)]
    half = (half + parts[2]) + (parts[0] + parts[1])
    return join_core(half, core)


def sum_all(gram):
    place = lax.axis_index("author")
    core, x = place % 2, place // 2
    half = split_core(gram, core)
    chunks = half.reshape(4, half.shape[0] // 4, half.shape[1])
    got = [hop_x(pick(chunks, (x + k) % 4), k) for k in (1, 3, 2)]
    part = (pick(chunks, x) + got[2]) + (got[0] + got[1])
    for hop in (hop_y, hop_z):
        got = [hop(part, k) for k in (1, 3, 2)]
        part = (part + got[2]) + (got[0] + got[1])
    ring = jnp.stack([part] + [hop_x(part, k) for k in (1, 2, 3)])
    half = jnp.take(ring, (x - jnp.arange(4)) % 4, axis=0).reshape(half.shape)
    return join_core(half, core)


def eliminate(strips):
    shape = strips[0].shape
    sub = lax.broadcasted_iota(jnp.int32, shape, 0)
    half = shape[1] // 2

    def column(strip, lane):
        return jnp.broadcast_to(strip[:, lane : lane + 1], shape)

    def row(strip, j):
        return jnp.broadcast_to(strip[j : j + 1, :], shape)

    for p in range(len(strips)):
        lead = strips[p]
        lanes = [half + 8 * p + j for j in range(8)]
        cols = [column(lead, lane) for lane in lanes]
        below = {i: [column(strips[i], lane) for lane in lanes] for i in range(p + 1, len(strips))}
        scale = jnp.zeros(shape, jnp.float32)
        for j in range(0, 8, 2):
            a, b, c = row(cols[j], j), row(cols[j + 1], j), row(cols[j + 1], j + 1)
            inv0 = 1.0 / a
            inv1 = a / (a * c - b * b)
            m0 = jnp.where(sub > j, cols[j] * inv0, 0.0)
            m1 = jnp.where(sub > j + 1, (cols[j + 1] - m0 * b) * inv1, 0.0)
            top0 = row(lead, j)
            top1 = row(lead, j + 1) - (b * inv0) * top0
            lead = (lead - m0 * top0) - m1 * top1
            scale = jnp.where(sub == j, lax.rsqrt(a), scale)
            scale = jnp.where(sub == j + 1, jnp.sqrt(inv1), scale)
            tops = []
            for k in range(j + 2, 8):
                u0 = row(cols[k], j)
                u1 = row(cols[k], j + 1) - (b * inv0) * u0
                cols[k] = (cols[k] - m0 * u0) - m1 * u1
                tops.append((u0, u1))
            for i, col in below.items():
                n0 = col[j] * inv0
                n1 = (col[j + 1] - n0 * b) * inv1
                for k, (u0, u1) in zip(range(j + 2, 8), tops):
                    col[k] = (col[k] - n0 * u0) - n1 * u1
                strips[i] = (strips[i] - n0 * top0) - n1 * top1
        strips[p] = lead * scale
    return strips


def whiten_kernel(g_ref, out_ref, s_ref, y_ref):
    n = g_ref.shape[0]
    g = g_ref[...]
    eye = lax.broadcasted_iota(jnp.int32, (n, n), 0) == lax.broadcasted_iota(jnp.int32, (n, n), 1)
    diag = jnp.where(eye, g, 0.0)
    across = lax.rsqrt(jnp.sum(diag, axis=0, keepdims=True))
    down = lax.rsqrt(jnp.sum(diag, axis=1, keepdims=True))
    s_ref[...] = g * across * down
    y_ref[...] = jnp.where(eye, 1.0, 0.0)
    lane = lax.broadcasted_iota(jnp.int32, (BLOCK, n), 1)
    def stage(at, carry):
        rows = pl.ds(pl.multiple_of(at * BLOCK, BLOCK), BLOCK)
        left, right = s_ref[rows, :], y_ref[rows, :]
        turned = pltpu.roll(left, lax.rem(n + BLOCK - at * BLOCK, n), 1)[:, : 2 * BLOCK]
        i0 = lax.broadcasted_iota(jnp.int32, turned.shape, 0)
        i1 = lax.broadcasted_iota(jnp.int32, turned.shape, 1)
        start = jnp.where(i1 < BLOCK, jnp.where(i0 == i1, 1.0, 0.0), turned)
        strips = eliminate([start[8 * i : 8 * i + 8] for i in range(BLOCK // 8)])
        inverse = jnp.concatenate(strips, axis=0)[:, :BLOCK]
        dot = lambda u, v, d: lax.dot_general(u, v, (((d,), (0,)), ((), ())), precision=HIGH, preferred_element_type=jnp.float32)
        left = dot(inverse, left, 1)
        right = dot(inverse, right, 1)
        rest = jnp.where(lane >= (at + 1) * BLOCK, left, 0.0)
        s_ref[...] -= dot(rest, left, 0)
        y_ref[...] -= dot(rest, right, 0)
        y_ref[rows, :] = right
        return carry
    lax.fori_loop(0, n // BLOCK, stage, 0)
    out_ref[...] = y_ref[...] * across


def whitener(gram):
    return pl.pallas_call(
        whiten_kernel,
        out_shape=jax.ShapeDtypeStruct(gram.shape, jnp.float32),
        scratch_shapes=[pltpu.VMEM(gram.shape, jnp.float32)] * 2,
        cost_estimate=pl.CostEstimate(flops=10**9, bytes_accessed=40 * 10**6, transcendentals=0),
        name="whitener",
    )(gram)


def apply_t(field, inverse, precision=MIDDLE):
    return lax.dot_general(
        field, inverse, (((1,), (1,)), ((), ())), precision=precision, preferred_element_type=jnp.float32
    )


def swap_word(parts):
    return lax.all_to_all(parts, "word", 0, 0)


def short(array):
    return array.astype(jnp.bfloat16)


def long(array):
    return array.astype(jnp.float32)


def shards(block_values, block_rows, block_cols, block_count, omega):
    values = block_values[0, 0]
    rows = block_rows[0, 0]
    cols = block_cols[0, 0]
    count = block_count[0, 0]
    size = values.shape[1]
    word_blocks = omega.shape[0] // size
    author_blocks = 32
    authors = author_blocks * size * lax.axis_size("author")
    words = word_blocks * size * lax.axis_size("word")
    wide = omega
    word_factor = None
    for turn in range(ITERS):
        terms = product(values, cols, rows, count, wide, author_blocks)
        y, copies = fold(swap_word(terms.reshape(16, -1, terms.shape[1])), word_factor)
        y_rows = swap_word(copies).reshape(terms.shape)
        terms = product_t(values, rows, cols, count, y_rows, word_blocks)
        z = long(lax.psum_scatter(terms, "author", scatter_dimension=0, tiled=True))
        author_factor = whitener(sum_author(gram_short(y_rows)) / authors)
        z = apply_t(z, author_factor)
        gram = sum_all(gram_of(z)) / words
        if turn + 1 < ITERS:
            wide = lax.all_gather(short(z), "author", axis=0, tiled=True)
            wide, gram = lax.optimization_barrier((wide, gram))
        word_factor = whitener(gram)
    author_basis = short(apply_t(y, author_factor))
    word_basis = short(apply_t(z, word_factor))
    return (author_basis, word_basis)


def solution(mesh):
    return jax.shard_map(
        shards,
        mesh=mesh,
        in_specs=(
            P("author", "word", None, None, None),
            P("author", "word", None),
            P("author", "word", None),
            P("author", "word"),
            P("word", None),
        ),
        out_specs=(P(("author", "word"), None), P(("word", "author"), None)),
        check_vma=False,
    )
```

```python
import jax
import jax.numpy as jnp
from jax import lax
from jax.experimental import pallas as pl
from jax.experimental.pallas import tpu as pltpu
from jax.sharding import PartitionSpec as P

ITERS = 2
GROUP = 16
CUT = 2048
BLOCK = 64
HIGH = lax.Precision.HIGHEST
MIDDLE = lax.Precision.HIGH


def product_kernel(src_ids, dst_ids, count, values, given, out, total, part, panel, part_sem, panel_sem):
    size = part.shape[1]
    groups = (count[0] + GROUP - 1) // GROUP

    def fetch(group):
        span = pl.ds(group * GROUP, GROUP)
        return pltpu.make_async_copy(values.at[span], part.at[span], part_sem.at[group])

    def start(group, carry):
        fetch(group).start()
        return carry

    def clear(index, carry):
        total[index] = jnp.zeros_like(total[index])
        return carry

    def work(group, carry):
        fetch(group).wait()
        first = group * GROUP
        prods = []
        for offset in range(GROUP):
            rows = pl.ds(pl.multiple_of(src_ids[first + offset] * size, size), size)
            prods.append(jnp.dot(part[first + offset], panel[rows, :], preferred_element_type=jnp.float32))
        for offset in range(GROUP):
            total[dst_ids[first + offset]] += prods[offset]
        return carry

    def emit(index, carry):
        out[pl.ds(pl.multiple_of(index * size, size), size), :] = total[index].astype(out.dtype)
        return carry

    moves = []
    for index in range(panel_sem.shape[0]):
        rows = pl.ds(index * CUT, CUT)
        moves.append(pltpu.make_async_copy(given.at[rows], panel.at[rows], panel_sem.at[index]))
    fetch(0).start()
    for move in moves:
        move.start()
    lax.fori_loop(1, groups, start, 0)
    lax.fori_loop(0, total.shape[0], clear, 0)
    for move in moves:
        move.wait()
    lax.fori_loop(0, groups, work, 0)
    lax.fori_loop(0, out.shape[0] // size, emit, 0)


def product_t_kernel(src_ids, dst_ids, count, values, panel, out, total, part, staged, part_sem, out_sem):
    size = part.shape[1]
    groups = (count[0] + GROUP - 1) // GROUP

    def fetch(group):
        span = pl.ds(group * GROUP, GROUP)
        return pltpu.make_async_copy(values.at[span], part.at[span], part_sem.at[group])

    def start(group, carry):
        fetch(group).start()
        return carry

    def clear(index, carry):
        total[index] = jnp.zeros_like(total[index])
        return carry

    def work(group, carry):
        fetch(group).wait()
        first = group * GROUP
        prods = []
        for offset in range(GROUP):
            rows = pl.ds(pl.multiple_of(src_ids[first + offset] * size, size), size)
            prods.append(
                lax.dot_general(
                    part[first + offset],
                    panel[rows, :],
                    (((0,), (0,)), ((), ())),
                    preferred_element_type=jnp.float32,
                )
            )
        for offset in range(GROUP):
            total[dst_ids[first + offset]] += prods[offset]
        return carry

    def emit(index, carry):
        staged[pl.ds(pl.multiple_of(index * size, size), size), :] = total[index].astype(staged.dtype)
        return carry

    lax.fori_loop(0, groups, start, 0)
    lax.fori_loop(0, total.shape[0], clear, 0)
    lax.fori_loop(0, groups, work, 0)
    blocks = out.shape[0] // size
    pieces = out_sem.shape[0]
    sends = []
    for piece in range(pieces):
        lax.fori_loop(piece * blocks // pieces, (piece + 1) * blocks // pieces, emit, 0)
        rows = pl.ds(piece * out.shape[0] // pieces, out.shape[0] // pieces)
        sends.append(pltpu.make_async_copy(staged.at[rows], out.at[rows], out_sem.at[piece]))
        sends[-1].start()
    for send in sends:
        send.wait()


def kernel_call(kernel, name, operands, specs, out, cap, size, scratch):
    rows, width = out.shape
    return pl.pallas_call(
        kernel,
        out_shape=out,
        in_specs=specs,
        out_specs=pl.BlockSpec(memory_space=pltpu.VMEM if name == "product" else pl.ANY),
        scratch_shapes=[
            pltpu.VMEM((rows // size + 1, size, width), jnp.float32),
            pltpu.VMEM((cap, size, size), jnp.bfloat16),
            *scratch,
        ],
        compiler_params=pltpu.CompilerParams(vmem_limit_bytes=36 * 1024 * 1024),
        cost_estimate=pl.CostEstimate(
            flops=4 * cap * size * size * width, bytes_accessed=20 * 1024 * 1024, transcendentals=0
        ),
        name=name,
    )(*operands)


def product(values, cols, rows, count, panel, out_blocks):
    cap, size, _ = values.shape
    width = panel.shape[1]
    rows = jnp.where(jnp.arange(cap, dtype=jnp.int32) < count, rows, out_blocks)
    smem = pl.BlockSpec(memory_space=pltpu.SMEM)
    whole = pl.BlockSpec(memory_space=pl.ANY)
    values = pltpu.with_memory_space_constraint(values, pltpu.HBM)
    panel = pltpu.with_memory_space_constraint(panel, pltpu.HBM)
    scratch = [
        pltpu.VMEM(panel.shape, jnp.bfloat16),
        pltpu.SemaphoreType.DMA((cap // GROUP,)),
        pltpu.SemaphoreType.DMA((panel.shape[0] // CUT,)),
    ]
    operands = (cols, rows, count.reshape(1), values, panel)
    specs = [smem] * 3 + [whole] * 2
    out = pltpu.VMEM((out_blocks * size, width), jnp.bfloat16)
    return kernel_call(product_kernel, "product", operands, specs, out, cap, size, scratch)


def product_t(values, rows, cols, count, panel, out_blocks):
    cap, size, _ = values.shape
    cols = jnp.where(jnp.arange(cap, dtype=jnp.int32) < count, cols, out_blocks)
    smem = pl.BlockSpec(memory_space=pltpu.SMEM)
    whole = pl.BlockSpec(memory_space=pl.ANY)
    vmem = pl.BlockSpec(memory_space=pltpu.VMEM)
    values = pltpu.with_memory_space_constraint(values, pltpu.HBM)
    out = pltpu.HBM((out_blocks * size, panel.shape[1]), jnp.bfloat16)
    scratch = [
        pltpu.VMEM(out.shape, jnp.bfloat16),
        pltpu.SemaphoreType.DMA((cap // GROUP,)),
        pltpu.SemaphoreType.DMA((8,)),
    ]
    operands = (rows, cols, count.reshape(1), values, panel)
    specs = [smem] * 3 + [whole, vmem]
    return kernel_call(product_t_kernel, "product_t", operands, specs, out, cap, size, scratch)


def fold_kernel(parts, factor, field, copies):
    total = parts[0].astype(jnp.float32)
    for index in range(1, parts.shape[0]):
        total += parts[index].astype(jnp.float32)
    if factor is not None:
        total = apply_t(total, factor[...], HIGH)
    field[...] = total
    short = total.astype(copies.dtype)
    for index in range(copies.shape[0]):
        copies[index] = short


def fold(parts, factor):
    vmem = pl.BlockSpec(memory_space=pltpu.VMEM)
    operands = (parts,) if factor is None else (parts, factor)
    kernel = fold_kernel if factor is not None else lambda p, f, c: fold_kernel(p, None, f, c)
    return pl.pallas_call(
        kernel,
        out_shape=(
            pltpu.VMEM(parts.shape[1:], jnp.float32),
            pltpu.VMEM(parts.shape, jnp.bfloat16),
        ),
        in_specs=[vmem] * len(operands),
        out_specs=(vmem, vmem),
        name="fold",
    )(*operands)


def gram_kernel(field, out):
    total = jnp.zeros(out.shape, jnp.float32)
    step = 512
    for start in range(0, field.shape[0], step):
        part = field[pl.ds(start, step), :]
        total += lax.dot_general(part, part, (((0,), (0,)), ((), ())), preferred_element_type=jnp.float32)
    out[...] = total


def gram_short(field):
    vmem = pl.BlockSpec(memory_space=pltpu.VMEM)
    return pl.pallas_call(
        gram_kernel,
        out_shape=jax.ShapeDtypeStruct((field.shape[1],) * 2, jnp.float32),
        in_specs=[vmem],
        out_specs=vmem,
        name="gram_short",
    )(field)


def gram_of(field):
    return lax.dot_general(
        field, field, (((0,), (0,)), ((), ())), precision=MIDDLE, preferred_element_type=jnp.float32
    )


def hop_core(array):
    return lax.ppermute(array, "author", [(i, i ^ 1) for i in range(8)])


def hop_x(array, k):
    return lax.ppermute(array, "author", [(i, (i + 2 * k) % 8) for i in range(8)])


def hop_y(array, k):
    return lax.ppermute(array, "word", [(i, (i + 4 * k) % 16) for i in range(16)])


def hop_z(array, k):
    return lax.ppermute(array, "word", [(i, (i // 4) * 4 + (i + k) % 4) for i in range(16)])


def pick(array, index):
    return lax.dynamic_index_in_dim(array, index, 0, keepdims=False)


def split_core(gram, core):
    halves = gram.reshape(2, gram.shape[0] // 2, gram.shape[1])
    return pick(halves, core) + hop_core(pick(halves, 1 - core))


def join_core(half, core):
    other = hop_core(half)
    return jnp.where(core == 0, jnp.concatenate([half, other]), jnp.concatenate([other, half]))


def sum_author(gram):
    core = lax.axis_index("author") % 2
    half = split_core(gram, core)
    parts = [hop_x(half, k) for k in (1, 3, 2)]
    half = (half + parts[2]) + (parts[0] + parts[1])
    return join_core(half, core)


def sum_all(gram):
    place = lax.axis_index("author")
    core, x = place % 2, place // 2
    half = split_core(gram, core)
    chunks = half.reshape(4, half.shape[0] // 4, half.shape[1])
    got = [hop_x(pick(chunks, (x + k) % 4), k) for k in (1, 3, 2)]
    part = (pick(chunks, x) + got[2]) + (got[0] + got[1])
    for hop in (hop_y, hop_z):
        got = [hop(part, k) for k in (1, 3, 2)]
        part = (part + got[2]) + (got[0] + got[1])
    ring = jnp.stack([part] + [hop_x(part, k) for k in (1, 2, 3)])
    half = jnp.take(ring, (x - jnp.arange(4)) % 4, axis=0).reshape(half.shape)
    return join_core(half, core)


def sum_all_swap(gram):
    axes = ("author", "word")
    devices = lax.axis_size(axes)
    parts = lax.all_to_all(gram.reshape(devices, -1, gram.shape[1]), axes, 0, 0)
    rows = jnp.sum(parts, axis=0)
    rows = jnp.broadcast_to(rows[None], (devices,) + rows.shape)
    return lax.all_to_all(rows, axes, 0, 0).reshape(gram.shape)


def eliminate(strips):
    shape = strips[0].shape
    sub = lax.broadcasted_iota(jnp.int32, shape, 0)
    half = shape[1] // 2

    def column(strip, lane):
        return jnp.broadcast_to(strip[:, lane : lane + 1], shape)

    def row(strip, j):
        return jnp.broadcast_to(strip[j : j + 1, :], shape)

    for p in range(len(strips)):
        lead = strips[p]
        lanes = [half + 8 * p + j for j in range(8)]
        cols = [column(lead, lane) for lane in lanes]
        below = {i: [column(strips[i], lane) for lane in lanes] for i in range(p + 1, len(strips))}
        scale = jnp.zeros(shape, jnp.float32)
        for j in range(0, 8, 2):
            a, b, c = row(cols[j], j), row(cols[j + 1], j), row(cols[j + 1], j + 1)
            inv0 = 1.0 / a
            inv1 = a / (a * c - b * b)
            m0 = jnp.where(sub > j, cols[j] * inv0, 0.0)
            m1 = jnp.where(sub > j + 1, (cols[j + 1] - m0 * b) * inv1, 0.0)
            top0 = row(lead, j)
            top1 = row(lead, j + 1) - (b * inv0) * top0
            lead = (lead - m0 * top0) - m1 * top1
            scale = jnp.where(sub == j, lax.rsqrt(a), scale)
            scale = jnp.where(sub == j + 1, jnp.sqrt(inv1), scale)
            tops = []
            for k in range(j + 2, 8):
                u0 = row(cols[k], j)
                u1 = row(cols[k], j + 1) - (b * inv0) * u0
                cols[k] = (cols[k] - m0 * u0) - m1 * u1
                tops.append((u0, u1))
            for i, col in below.items():
                n0 = col[j] * inv0
                n1 = (col[j + 1] - n0 * b) * inv1
                for k, (u0, u1) in zip(range(j + 2, 8), tops):
                    col[k] = (col[k] - n0 * u0) - n1 * u1
                strips[i] = (strips[i] - n0 * top0) - n1 * top1
        strips[p] = lead * scale
    return strips


def whiten_kernel(g_ref, out_ref, s_ref, y_ref):
    n = g_ref.shape[0]
    g = g_ref[...]
    eye = lax.broadcasted_iota(jnp.int32, (n, n), 0) == lax.broadcasted_iota(jnp.int32, (n, n), 1)
    diag = jnp.where(eye, g, 0.0)
    across = lax.rsqrt(jnp.sum(diag, axis=0, keepdims=True))
    down = lax.rsqrt(jnp.sum(diag, axis=1, keepdims=True))
    s_ref[...] = g * across * down
    y_ref[...] = jnp.where(eye, 1.0, 0.0)
    lane = lax.broadcasted_iota(jnp.int32, (BLOCK, n), 1)
    def stage(at, carry):
        rows = pl.ds(pl.multiple_of(at * BLOCK, BLOCK), BLOCK)
        left, right = s_ref[rows, :], y_ref[rows, :]
        turned = pltpu.roll(left, lax.rem(n + BLOCK - at * BLOCK, n), 1)[:, : 2 * BLOCK]
        i0 = lax.broadcasted_iota(jnp.int32, turned.shape, 0)
        i1 = lax.broadcasted_iota(jnp.int32, turned.shape, 1)
        start = jnp.where(i1 < BLOCK, jnp.where(i0 == i1, 1.0, 0.0), turned)
        strips = eliminate([start[8 * i : 8 * i + 8] for i in range(BLOCK // 8)])
        inverse = jnp.concatenate(strips, axis=0)[:, :BLOCK]
        dot = lambda u, v, d: lax.dot_general(u, v, (((d,), (0,)), ((), ())), precision=HIGH, preferred_element_type=jnp.float32)
        left = dot(inverse, left, 1)
        right = dot(inverse, right, 1)

        @pl.when(at + 1 < n // BLOCK)
        def _():
            rest = jnp.where(lane >= (at + 1) * BLOCK, left, 0.0)
            s_ref[...] -= dot(rest, left, 0)
            y_ref[...] -= dot(rest, right, 0)

        y_ref[rows, :] = right
        return carry
    lax.fori_loop(0, n // BLOCK, stage, 0)
    out_ref[...] = y_ref[...] * across


def whitener(gram):
    return pl.pallas_call(
        whiten_kernel,
        out_shape=jax.ShapeDtypeStruct(gram.shape, jnp.float32),
        scratch_shapes=[pltpu.VMEM(gram.shape, jnp.float32)] * 2,
        cost_estimate=pl.CostEstimate(flops=10**9, bytes_accessed=40 * 10**6, transcendentals=0),
        name="whitener",
    )(gram)


def apply_t(field, inverse, precision=MIDDLE):
    return lax.dot_general(
        field, inverse, (((1,), (1,)), ((), ())), precision=precision, preferred_element_type=jnp.float32
    )


def swap_word(parts):
    return lax.all_to_all(parts, "word", 0, 0)


def short(array):
    return array.astype(jnp.bfloat16)


def long(array):
    return array.astype(jnp.float32)


def shards(block_values, block_rows, block_cols, block_count, omega):
    values = block_values[0, 0]
    rows = block_rows[0, 0]
    cols = block_cols[0, 0]
    count = block_count[0, 0]
    size = values.shape[1]
    word_blocks = omega.shape[0] // size
    author_blocks = 32
    authors = author_blocks * size * lax.axis_size("author")
    words = word_blocks * size * lax.axis_size("word")
    wide = omega
    word_factor = None
    for turn in range(ITERS):
        terms = product(values, cols, rows, count, wide, author_blocks)
        y, copies = fold(swap_word(terms.reshape(16, -1, terms.shape[1])), word_factor)
        y_rows = swap_word(copies).reshape(terms.shape)
        terms = product_t(values, rows, cols, count, y_rows, word_blocks)
        z = long(lax.psum_scatter(terms, "author", scatter_dimension=0, tiled=True))
        author_factor = whitener(sum_author(gram_short(y_rows)) / authors)
        z = apply_t(z, author_factor)
        gram = (sum_all if turn + 1 < ITERS else sum_all_swap)(gram_of(z)) / words
        if turn + 1 < ITERS:
            wide = lax.all_gather(short(z), "author", axis=0, tiled=True)
            wide, gram = lax.optimization_barrier((wide, gram))
        word_factor = whitener(gram)
    author_basis = short(apply_t(y, author_factor))
    word_basis = short(apply_t(z, word_factor))
    return (author_basis, word_basis)


def solution(mesh):
    return jax.shard_map(
        shards,
        mesh=mesh,
        in_specs=(
            P("author", "word", None, None, None),
            P("author", "word", None),
            P("author", "word", None),
            P("author", "word"),
            P("word", None),
        ),
        out_specs=(P(("author", "word"), None), P(("word", "author"), None)),
        check_vma=False,
    )
```

```python
import jax
import jax.numpy as jnp
from jax import lax
from jax.experimental import pallas as pl
from jax.experimental.pallas import tpu as pltpu
from jax.sharding import PartitionSpec as P

ITERS = 2
GROUP = 16
CUT = 2048
BLOCK = 64
HIGH = lax.Precision.HIGHEST
MIDDLE = lax.Precision.HIGH


def product_kernel(
    src_ids, dst_ids, count, core, values, given, out, total, part, panel, part_sem, panel_sem
):
    size = part.shape[1]
    groups = (count[0] + GROUP - 1) // GROUP

    def fetch(group):
        span = pl.ds(group * GROUP, GROUP)
        return pltpu.make_async_copy(values.at[span], part.at[span], part_sem.at[group])

    def start(group, carry):
        fetch(group).start()
        return carry

    def clear(index, carry):
        total[index] = jnp.zeros_like(total[index])
        return carry

    def work(group, carry):
        fetch(group).wait()
        first = group * GROUP
        prods = []
        for offset in range(GROUP):
            rows = pl.ds(pl.multiple_of(src_ids[first + offset] * size, size), size)
            prods.append(jnp.dot(part[first + offset], panel[rows, :], preferred_element_type=jnp.float32))
        for offset in range(GROUP):
            total[dst_ids[first + offset]] += prods[offset]
        return carry

    def emit(index, carry):
        share, row = index // 2, index % 2
        place = jnp.where(core[0] == 0, share % 4 * 4 + share // 4, share) * 2 + row
        out[pl.ds(pl.multiple_of(place * size, size), size), :] = total[index].astype(out.dtype)
        return carry

    moves = []
    for index in range(panel_sem.shape[0]):
        rows = pl.ds(index * CUT, CUT)
        moves.append(pltpu.make_async_copy(given.at[rows], panel.at[rows], panel_sem.at[index]))
    fetch(0).start()
    for move in moves:
        move.start()
    lax.fori_loop(1, groups, start, 0)
    lax.fori_loop(0, total.shape[0], clear, 0)
    for move in moves:
        move.wait()
    lax.fori_loop(0, groups, work, 0)
    lax.fori_loop(0, out.shape[0] // size, emit, 0)


def product_t_kernel(src_ids, dst_ids, count, values, panel, out, total, part, staged, part_sem, out_sem):
    size = part.shape[1]
    groups = (count[0] + GROUP - 1) // GROUP

    def fetch(group):
        span = pl.ds(group * GROUP, GROUP)
        return pltpu.make_async_copy(values.at[span], part.at[span], part_sem.at[group])

    def start(group, carry):
        fetch(group).start()
        return carry

    def clear(index, carry):
        total[index] = jnp.zeros_like(total[index])
        return carry

    def work(group, carry):
        fetch(group).wait()
        first = group * GROUP
        prods = []
        for offset in range(GROUP):
            rows = pl.ds(pl.multiple_of(src_ids[first + offset] * size, size), size)
            prods.append(
                lax.dot_general(
                    part[first + offset],
                    panel[rows, :],
                    (((0,), (0,)), ((), ())),
                    preferred_element_type=jnp.float32,
                )
            )
        for offset in range(GROUP):
            total[dst_ids[first + offset]] += prods[offset]
        return carry

    def emit(index, carry):
        staged[pl.ds(pl.multiple_of(index * size, size), size), :] = total[index].astype(staged.dtype)
        return carry

    lax.fori_loop(0, groups, start, 0)
    lax.fori_loop(0, total.shape[0], clear, 0)
    lax.fori_loop(0, groups, work, 0)
    blocks = out.shape[0] // size
    pieces = out_sem.shape[0]
    sends = []
    for piece in range(pieces):
        lax.fori_loop(piece * blocks // pieces, (piece + 1) * blocks // pieces, emit, 0)
        rows = pl.ds(piece * out.shape[0] // pieces, out.shape[0] // pieces)
        sends.append(pltpu.make_async_copy(staged.at[rows], out.at[rows], out_sem.at[piece]))
        sends[-1].start()
    for send in sends:
        send.wait()


def kernel_call(kernel, name, operands, specs, out, cap, size, scratch):
    rows, width = out.shape
    return pl.pallas_call(
        kernel,
        out_shape=out,
        in_specs=specs,
        out_specs=pl.BlockSpec(memory_space=pltpu.VMEM if name == "product" else pl.ANY),
        scratch_shapes=[
            pltpu.VMEM((rows // size + 1, size, width), jnp.float32),
            pltpu.VMEM((cap, size, size), jnp.bfloat16),
            *scratch,
        ],
        compiler_params=pltpu.CompilerParams(vmem_limit_bytes=36 * 1024 * 1024),
        cost_estimate=pl.CostEstimate(
            flops=4 * cap * size * size * width, bytes_accessed=20 * 1024 * 1024, transcendentals=0
        ),
        name=name,
    )(*operands)


def product(values, cols, rows, count, core, panel, out_blocks):
    cap, size, _ = values.shape
    width = panel.shape[1]
    rows = jnp.where(jnp.arange(cap, dtype=jnp.int32) < count, rows, out_blocks)
    smem = pl.BlockSpec(memory_space=pltpu.SMEM)
    whole = pl.BlockSpec(memory_space=pl.ANY)
    values = pltpu.with_memory_space_constraint(values, pltpu.HBM)
    panel = pltpu.with_memory_space_constraint(panel, pltpu.HBM)
    scratch = [
        pltpu.VMEM(panel.shape, jnp.bfloat16),
        pltpu.SemaphoreType.DMA((cap // GROUP,)),
        pltpu.SemaphoreType.DMA((panel.shape[0] // CUT,)),
    ]
    operands = (cols, rows, count.reshape(1), core.reshape(1), values, panel)
    specs = [smem] * 4 + [whole] * 2
    out = pltpu.VMEM((out_blocks * size, width), jnp.bfloat16)
    return kernel_call(product_kernel, "product", operands, specs, out, cap, size, scratch)


def product_t(values, rows, cols, count, panel, out_blocks):
    cap, size, _ = values.shape
    cols = jnp.where(jnp.arange(cap, dtype=jnp.int32) < count, cols, out_blocks)
    smem = pl.BlockSpec(memory_space=pltpu.SMEM)
    whole = pl.BlockSpec(memory_space=pl.ANY)
    vmem = pl.BlockSpec(memory_space=pltpu.VMEM)
    values = pltpu.with_memory_space_constraint(values, pltpu.HBM)
    out = pltpu.HBM((out_blocks * size, panel.shape[1]), jnp.bfloat16)
    scratch = [
        pltpu.VMEM(out.shape, jnp.bfloat16),
        pltpu.SemaphoreType.DMA((cap // GROUP,)),
        pltpu.SemaphoreType.DMA((8,)),
    ]
    operands = (rows, cols, count.reshape(1), values, panel)
    specs = [smem] * 3 + [whole, vmem]
    return kernel_call(product_t_kernel, "product_t", operands, specs, out, cap, size, scratch)


def fold_kernel(parts, factor, field, brief):
    total = parts[0][...].astype(jnp.float32)
    for part in parts[1:]:
        total += part[...].astype(jnp.float32)
    if factor is not None:
        total = apply_t(total, factor[...], HIGH)
    field[...] = total
    brief[...] = total.astype(brief.dtype)


def fold(parts, factor):
    vmem = pl.BlockSpec(memory_space=pltpu.VMEM)
    count = len(parts)
    operands = list(parts) + ([] if factor is None else [factor])

    def kernel(*refs):
        fold_kernel(refs[:count], refs[count] if factor is not None else None, *refs[-2:])

    return pl.pallas_call(
        kernel,
        out_shape=(
            jax.ShapeDtypeStruct(parts[0].shape, jnp.float32),
            jax.ShapeDtypeStruct(parts[0].shape, jnp.bfloat16),
        ),
        in_specs=[vmem] * len(operands),
        out_specs=(vmem, vmem),
        name="fold",
    )(*operands)


def gram_kernel(field, out):
    total = jnp.zeros(out.shape, jnp.float32)
    step = 512
    for start in range(0, field.shape[0], step):
        part = field[pl.ds(start, step), :]
        total += lax.dot_general(part, part, (((0,), (0,)), ((), ())), preferred_element_type=jnp.float32)
    out[...] = total


def gram_short(field):
    vmem = pl.BlockSpec(memory_space=pltpu.VMEM)
    return pl.pallas_call(
        gram_kernel,
        out_shape=jax.ShapeDtypeStruct((field.shape[1],) * 2, jnp.float32),
        in_specs=[vmem],
        out_specs=vmem,
        name="gram_short",
    )(field)


def gram_of(field):
    return lax.dot_general(
        field, field, (((0,), (0,)), ((), ())), precision=MIDDLE, preferred_element_type=jnp.float32
    )


def hop_core(array):
    return lax.ppermute(array, "author", [(i, i ^ 1) for i in range(8)])


def hop_x(array, k):
    return lax.ppermute(array, "author", [(i, (i + 2 * k) % 8) for i in range(8)])


def hop_y(array, k):
    return lax.ppermute(array, "word", [(i, (i + 4 * k) % 16) for i in range(16)])


def hop_z(array, k):
    return lax.ppermute(array, "word", [(i, (i // 4) * 4 + (i + k) % 4) for i in range(16)])


def pick(array, index):
    return lax.dynamic_index_in_dim(array, index, 0, keepdims=False)


def split_core(gram, core):
    halves = gram.reshape(2, gram.shape[0] // 2, gram.shape[1])
    return pick(halves, core) + hop_core(pick(halves, 1 - core))


def join_core(half, core):
    other = hop_core(half)
    return jnp.where(core == 0, jnp.concatenate([half, other]), jnp.concatenate([other, half]))


def sum_author(gram):
    core = lax.axis_index("author") % 2
    half = split_core(gram, core)
    parts = [hop_x(half, k) for k in (1, 3, 2)]
    half = (half + parts[2]) + (parts[0] + parts[1])
    return join_core(half, core)


def sum_all(gram):
    place = lax.axis_index("author")
    core, x = place % 2, place // 2
    half = split_core(gram, core)
    chunks = half.reshape(4, half.shape[0] // 4, half.shape[1])
    got = [hop_x(pick(chunks, (x + k) % 4), k) for k in (1, 3, 2)]
    part = (pick(chunks, x) + got[2]) + (got[0] + got[1])
    for hop in (hop_y, hop_z):
        got = [hop(part, k) for k in (1, 3, 2)]
        part = (part + got[2]) + (got[0] + got[1])
    ring = jnp.stack([part] + [hop_x(part, k) for k in (1, 2, 3)])
    half = jnp.take(ring, (x - jnp.arange(4)) % 4, axis=0).reshape(half.shape)
    return join_core(half, core)


def sum_all_swap(gram):
    axes = ("author", "word")
    devices = lax.axis_size(axes)
    parts = lax.all_to_all(gram.reshape(devices, -1, gram.shape[1]), axes, 0, 0)
    rows = jnp.sum(parts, axis=0)
    rows = jnp.broadcast_to(rows[None], (devices,) + rows.shape)
    return lax.all_to_all(rows, axes, 0, 0).reshape(gram.shape)


def eliminate(strips):
    shape = strips[0].shape
    sub = lax.broadcasted_iota(jnp.int32, shape, 0)
    half = shape[1] // 2

    def column(strip, lane):
        return jnp.broadcast_to(strip[:, lane : lane + 1], shape)

    def row(strip, j):
        return jnp.broadcast_to(strip[j : j + 1, :], shape)

    for p in range(len(strips)):
        lead = strips[p]
        lanes = [half + 8 * p + j for j in range(8)]
        cols = [column(lead, lane) for lane in lanes]
        below = {i: [column(strips[i], lane) for lane in lanes] for i in range(p + 1, len(strips))}
        scale = jnp.zeros(shape, jnp.float32)
        for j in range(0, 8, 2):
            a, b, c = row(cols[j], j), row(cols[j + 1], j), row(cols[j + 1], j + 1)
            inv0 = 1.0 / a
            inv1 = a / (a * c - b * b)
            m0 = jnp.where(sub > j, cols[j] * inv0, 0.0)
            m1 = jnp.where(sub > j + 1, (cols[j + 1] - m0 * b) * inv1, 0.0)
            top0 = row(lead, j)
            top1 = row(lead, j + 1) - (b * inv0) * top0
            lead = (lead - m0 * top0) - m1 * top1
            scale = jnp.where(sub == j, lax.rsqrt(a), scale)
            scale = jnp.where(sub == j + 1, jnp.sqrt(inv1), scale)
            tops = []
            for k in range(j + 2, 8):
                u0 = row(cols[k], j)
                u1 = row(cols[k], j + 1) - (b * inv0) * u0
                cols[k] = (cols[k] - m0 * u0) - m1 * u1
                tops.append((u0, u1))
            for i, col in below.items():
                n0 = col[j] * inv0
                n1 = (col[j + 1] - n0 * b) * inv1
                for k, (u0, u1) in zip(range(j + 2, 8), tops):
                    col[k] = (col[k] - n0 * u0) - n1 * u1
                strips[i] = (strips[i] - n0 * top0) - n1 * top1
        strips[p] = lead * scale
    return strips


def whiten_kernel(g_ref, out_ref, s_ref, y_ref):
    n = g_ref.shape[0]
    g = g_ref[...]
    eye = lax.broadcasted_iota(jnp.int32, (n, n), 0) == lax.broadcasted_iota(jnp.int32, (n, n), 1)
    diag = jnp.where(eye, g, 0.0)
    across = lax.rsqrt(jnp.sum(diag, axis=0, keepdims=True))
    down = lax.rsqrt(jnp.sum(diag, axis=1, keepdims=True))
    s_ref[...] = g * across * down
    y_ref[...] = jnp.where(eye, 1.0, 0.0)
    lane = lax.broadcasted_iota(jnp.int32, (BLOCK, n), 1)
    def stage(at, carry):
        rows = pl.ds(pl.multiple_of(at * BLOCK, BLOCK), BLOCK)
        left, right = s_ref[rows, :], y_ref[rows, :]
        turned = pltpu.roll(left, lax.rem(n + BLOCK - at * BLOCK, n), 1)[:, : 2 * BLOCK]
        i0 = lax.broadcasted_iota(jnp.int32, turned.shape, 0)
        i1 = lax.broadcasted_iota(jnp.int32, turned.shape, 1)
        start = jnp.where(i1 < BLOCK, jnp.where(i0 == i1, 1.0, 0.0), turned)
        strips = eliminate([start[8 * i : 8 * i + 8] for i in range(BLOCK // 8)])
        inverse = jnp.concatenate(strips, axis=0)[:, :BLOCK]
        dot = lambda u, v, d: lax.dot_general(u, v, (((d,), (0,)), ((), ())), precision=HIGH, preferred_element_type=jnp.float32)
        left = dot(inverse, left, 1)
        right = dot(inverse, right, 1)

        @pl.when(at + 1 < n // BLOCK)
        def _():
            rest = jnp.where(lane >= (at + 1) * BLOCK, left, 0.0)
            s_ref[...] -= dot(rest, left, 0)
            y_ref[...] -= dot(rest, right, 0)

        y_ref[rows, :] = right
        return carry
    lax.fori_loop(0, n // BLOCK, stage, 0)
    out_ref[...] = y_ref[...] * across


def whitener(gram):
    return pl.pallas_call(
        whiten_kernel,
        out_shape=jax.ShapeDtypeStruct(gram.shape, jnp.float32),
        scratch_shapes=[pltpu.VMEM(gram.shape, jnp.float32)] * 2,
        cost_estimate=pl.CostEstimate(flops=10**9, bytes_accessed=40 * 10**6, transcendentals=0),
        name="whitener",
    )(gram)


def apply_t(field, inverse, precision=MIDDLE):
    return lax.dot_general(
        field, inverse, (((1,), (1,)), ((), ())), precision=precision, preferred_element_type=jnp.float32
    )


def short(array):
    return array.astype(jnp.bfloat16)


def long(array):
    return array.astype(jnp.float32)


def ring_places():
    core = lax.axis_index("author") % 2
    y, z = lax.axis_index("word") // 4, lax.axis_index("word") % 4
    return core, jnp.where(core == 0, z, y), jnp.where(core == 0, y, z)


def hop_ring(array, ring, k):
    pairs = []
    for device in range(128):
        core, y, z = device // 16 % 2, device % 16 // 4, device % 4
        if core == ring:
            z = (z + k) % 4
        else:
            y = (y + k) % 4
        pairs.append((device, device // 16 * 16 + y * 4 + z))
    return lax.ppermute(array, ("author", "word"), pairs)


def scatter_word(terms):
    _, one, two = ring_places()
    terms = terms.reshape(4, 4, -1, terms.shape[1])
    got = [hop_ring(pick(terms, (one + k) % 4), 0, k) for k in (2, 1, 3)]
    terms = short(long(pick(terms, one)) + long(got[0]) + long(got[1]) + long(got[2]))
    got = [hop_ring(pick(terms, (two + k) % 4), 1, k) for k in (2, 1, 3)]
    return [pick(terms, two)] + got


def gather_word(share):
    line = jnp.stack([share] + [hop_ring(share, 1, k) for k in (1, 2, 3)])
    return jnp.concatenate([line] + [hop_ring(line, 0, k) for k in (1, 2, 3)])


def ring_rows(rows):
    core, one, two = ring_places()
    share = rows // 2
    y, z = share // 4, share % 4
    first, second = jnp.where(core == 0, z, y), jnp.where(core == 0, y, z)
    return ((one - first) % 4 * 4 + (two - second) % 4) * 2 + rows % 2


def shards(block_values, block_rows, block_cols, block_count, omega):
    values = block_values[0, 0]
    rows = block_rows[0, 0]
    cols = block_cols[0, 0]
    count = block_count[0, 0]
    size = values.shape[1]
    word_blocks = omega.shape[0] // size
    author_blocks = 32
    authors = author_blocks * size * lax.axis_size("author")
    words = word_blocks * size * lax.axis_size("word")
    wide = omega
    word_factor = None
    for turn in range(ITERS):
        terms = product(values, cols, rows, count, ring_places()[0], wide, author_blocks)
        y, brief = fold(scatter_word(terms), word_factor)
        y_rows = gather_word(brief).reshape(terms.shape)
        terms = product_t(values, ring_rows(rows), cols, count, y_rows, word_blocks)
        z = long(lax.psum_scatter(terms, "author", scatter_dimension=0, tiled=True))
        author_factor = whitener(sum_author(gram_short(y_rows)) / authors)
        z = apply_t(z, author_factor)
        gram = (sum_all if turn + 1 < ITERS else sum_all_swap)(gram_of(z)) / words
        if turn + 1 < ITERS:
            wide = lax.all_gather(short(z), "author", axis=0, tiled=True)
            wide, gram = lax.optimization_barrier((wide, gram))
        word_factor = whitener(gram)
    author_basis = short(apply_t(y, author_factor))
    word_basis = short(apply_t(z, word_factor))
    return (author_basis, word_basis)


def solution(mesh):
    return jax.shard_map(
        shards,
        mesh=mesh,
        in_specs=(
            P("author", "word", None, None, None),
            P("author", "word", None),
            P("author", "word", None),
            P("author", "word"),
            P("word", None),
        ),
        out_specs=(P(("author", "word"), None), P(("word", "author"), None)),
        check_vma=False,
    )
```

```python
import jax
import jax.numpy as jnp
from jax import lax
from jax.experimental import pallas as pl
from jax.experimental.pallas import tpu as pltpu
from jax.sharding import PartitionSpec as P

ITERS = 2
GROUP = 16
CUT = 2048
BLOCK = 64
HIGH = lax.Precision.HIGHEST
MIDDLE = lax.Precision.HIGH


def product_kernel(
    src_ids, dst_ids, count, core, values, given, out, total, part, panel, part_sem, panel_sem
):
    size = part.shape[1]
    groups = (count[0] + GROUP - 1) // GROUP

    def fetch(group):
        span = pl.ds(group * GROUP, GROUP)
        return pltpu.make_async_copy(values.at[span], part.at[span], part_sem.at[group])

    def start(group, carry):
        fetch(group).start()
        return carry

    def clear(index, carry):
        total[index] = jnp.zeros_like(total[index])
        return carry

    def work(group, carry):
        fetch(group).wait()
        first = group * GROUP
        prods = []
        for offset in range(GROUP):
            rows = pl.ds(pl.multiple_of(src_ids[first + offset] * size, size), size)
            prods.append(jnp.dot(part[first + offset], panel[rows, :], preferred_element_type=jnp.float32))
        for offset in range(GROUP):
            total[dst_ids[first + offset]] += prods[offset]
        return carry

    def emit(index, carry):
        share, row = index // 2, index % 2
        place = jnp.where(core[0] == 0, share % 4 * 4 + share // 4, share) * 2 + row
        out[pl.ds(pl.multiple_of(place * size, size), size), :] = total[index].astype(out.dtype)
        return carry

    moves = []
    for index in range(panel_sem.shape[0]):
        rows = pl.ds(index * CUT, CUT)
        moves.append(pltpu.make_async_copy(given.at[rows], panel.at[rows], panel_sem.at[index]))
    fetch(0).start()
    for move in moves:
        move.start()
    lax.fori_loop(1, groups, start, 0)
    lax.fori_loop(0, total.shape[0], clear, 0)
    for move in moves:
        move.wait()
    lax.fori_loop(0, groups, work, 0)
    lax.fori_loop(0, out.shape[0] // size, emit, 0)


def product_t_kernel(src_ids, dst_ids, count, values, panel, out, total, part, staged, part_sem, out_sem):
    size = part.shape[1]
    groups = (count[0] + GROUP - 1) // GROUP

    def fetch(group):
        span = pl.ds(group * GROUP, GROUP)
        return pltpu.make_async_copy(values.at[span], part.at[span], part_sem.at[group])

    def start(group, carry):
        fetch(group).start()
        return carry

    def clear(index, carry):
        total[index] = jnp.zeros_like(total[index])
        return carry

    def work(group, carry):
        fetch(group).wait()
        first = group * GROUP
        prods = []
        for offset in range(GROUP):
            rows = pl.ds(pl.multiple_of(src_ids[first + offset] * size, size), size)
            prods.append(
                lax.dot_general(
                    part[first + offset],
                    panel[rows, :],
                    (((0,), (0,)), ((), ())),
                    preferred_element_type=jnp.float32,
                )
            )
        for offset in range(GROUP):
            total[dst_ids[first + offset]] += prods[offset]
        return carry

    def emit(index, carry):
        staged[pl.ds(pl.multiple_of(index * size, size), size), :] = total[index].astype(staged.dtype)
        return carry

    lax.fori_loop(0, groups, start, 0)
    lax.fori_loop(0, total.shape[0], clear, 0)
    lax.fori_loop(0, groups, work, 0)
    blocks = out.shape[0] // size
    pieces = out_sem.shape[0]
    sends = []
    for piece in range(pieces):
        lax.fori_loop(piece * blocks // pieces, (piece + 1) * blocks // pieces, emit, 0)
        rows = pl.ds(piece * out.shape[0] // pieces, out.shape[0] // pieces)
        sends.append(pltpu.make_async_copy(staged.at[rows], out.at[rows], out_sem.at[piece]))
        sends[-1].start()
    for send in sends:
        send.wait()


def kernel_call(kernel, name, operands, specs, out, cap, size, scratch):
    rows, width = out.shape
    return pl.pallas_call(
        kernel,
        out_shape=out,
        in_specs=specs,
        out_specs=pl.BlockSpec(memory_space=pltpu.VMEM if name == "product" else pl.ANY),
        scratch_shapes=[
            pltpu.VMEM((rows // size + 1, size, width), jnp.float32),
            pltpu.VMEM((cap, size, size), jnp.bfloat16),
            *scratch,
        ],
        compiler_params=pltpu.CompilerParams(vmem_limit_bytes=36 * 1024 * 1024),
        cost_estimate=pl.CostEstimate(
            flops=4 * cap * size * size * width, bytes_accessed=20 * 1024 * 1024, transcendentals=0
        ),
        name=name,
    )(*operands)


def product(values, cols, rows, count, core, panel, out_blocks):
    cap, size, _ = values.shape
    width = panel.shape[1]
    rows = jnp.where(jnp.arange(cap, dtype=jnp.int32) < count, rows, out_blocks)
    smem = pl.BlockSpec(memory_space=pltpu.SMEM)
    whole = pl.BlockSpec(memory_space=pl.ANY)
    values = pltpu.with_memory_space_constraint(values, pltpu.HBM)
    panel = pltpu.with_memory_space_constraint(panel, pltpu.HBM)
    scratch = [
        pltpu.VMEM(panel.shape, jnp.bfloat16),
        pltpu.SemaphoreType.DMA((cap // GROUP,)),
        pltpu.SemaphoreType.DMA((panel.shape[0] // CUT,)),
    ]
    operands = (cols, rows, count.reshape(1), core.reshape(1), values, panel)
    specs = [smem] * 4 + [whole] * 2
    out = pltpu.VMEM((out_blocks * size, width), jnp.bfloat16)
    return kernel_call(product_kernel, "product", operands, specs, out, cap, size, scratch)


def product_t(values, rows, cols, count, panel, out_blocks):
    cap, size, _ = values.shape
    cols = jnp.where(jnp.arange(cap, dtype=jnp.int32) < count, cols, out_blocks)
    smem = pl.BlockSpec(memory_space=pltpu.SMEM)
    whole = pl.BlockSpec(memory_space=pl.ANY)
    vmem = pl.BlockSpec(memory_space=pltpu.VMEM)
    values = pltpu.with_memory_space_constraint(values, pltpu.HBM)
    out = pltpu.HBM((out_blocks * size, panel.shape[1]), jnp.bfloat16)
    scratch = [
        pltpu.VMEM(out.shape, jnp.bfloat16),
        pltpu.SemaphoreType.DMA((cap // GROUP,)),
        pltpu.SemaphoreType.DMA((8,)),
    ]
    operands = (rows, cols, count.reshape(1), values, panel)
    specs = [smem] * 3 + [whole, vmem]
    return kernel_call(product_t_kernel, "product_t", operands, specs, out, cap, size, scratch)


def fold_kernel(parts, factor, field, brief):
    total = parts[0][...].astype(jnp.float32)
    for part in parts[1:]:
        total += part[...].astype(jnp.float32)
    if factor is not None:
        total = apply_t(total, factor[...], HIGH)
    field[...] = total
    brief[...] = total.astype(brief.dtype)


def fold(parts, factor):
    vmem = pl.BlockSpec(memory_space=pltpu.VMEM)
    count = len(parts)
    operands = list(parts) + ([] if factor is None else [factor])

    def kernel(*refs):
        fold_kernel(refs[:count], refs[count] if factor is not None else None, *refs[-2:])

    return pl.pallas_call(
        kernel,
        out_shape=(
            jax.ShapeDtypeStruct(parts[0].shape, jnp.float32),
            jax.ShapeDtypeStruct(parts[0].shape, jnp.bfloat16),
        ),
        in_specs=[vmem] * len(operands),
        out_specs=(vmem, vmem),
        name="fold",
    )(*operands)


def gram_kernel(field, out):
    total = jnp.zeros(out.shape, jnp.float32)
    step = 512
    for start in range(0, field.shape[0], step):
        part = field[pl.ds(start, step), :]
        total += lax.dot_general(part, part, (((0,), (0,)), ((), ())), preferred_element_type=jnp.float32)
    out[...] = total


def gram_short(field):
    vmem = pl.BlockSpec(memory_space=pltpu.VMEM)
    return pl.pallas_call(
        gram_kernel,
        out_shape=jax.ShapeDtypeStruct((field.shape[1],) * 2, jnp.float32),
        in_specs=[vmem],
        out_specs=vmem,
        name="gram_short",
    )(field)


def gram_of(field):
    return lax.dot_general(
        field, field, (((0,), (0,)), ((), ())), precision=MIDDLE, preferred_element_type=jnp.float32
    )


def hop_core(array):
    return lax.ppermute(array, "author", [(i, i ^ 1) for i in range(8)])


def hop_x(array, k):
    return lax.ppermute(array, "author", [(i, (i + 2 * k) % 8) for i in range(8)])


def hop_y(array, k):
    return lax.ppermute(array, "word", [(i, (i + 4 * k) % 16) for i in range(16)])


def hop_z(array, k):
    return lax.ppermute(array, "word", [(i, (i // 4) * 4 + (i + k) % 4) for i in range(16)])


def pick(array, index):
    return lax.dynamic_index_in_dim(array, index, 0, keepdims=False)


def split_core(gram, core):
    halves = gram.reshape(2, gram.shape[0] // 2, gram.shape[1])
    return pick(halves, core) + hop_core(pick(halves, 1 - core))


def join_core(half, core):
    other = hop_core(half)
    return jnp.where(core == 0, jnp.concatenate([half, other]), jnp.concatenate([other, half]))


def sum_author(gram):
    core = lax.axis_index("author") % 2
    half = split_core(gram, core)
    parts = [hop_x(half, k) for k in (1, 3, 2)]
    half = (half + parts[2]) + (parts[0] + parts[1])
    return join_core(half, core)


def sum_all(gram):
    place = lax.axis_index("author")
    core, x = place % 2, place // 2
    half = split_core(gram, core)
    chunks = half.reshape(4, half.shape[0] // 4, half.shape[1])
    got = [hop_x(pick(chunks, (x + k) % 4), k) for k in (1, 3, 2)]
    part = (pick(chunks, x) + got[2]) + (got[0] + got[1])
    for hop in (hop_y, hop_z):
        got = [hop(part, k) for k in (1, 3, 2)]
        part = (part + got[2]) + (got[0] + got[1])
    ring = jnp.stack([part] + [hop_x(part, k) for k in (1, 2, 3)])
    half = jnp.take(ring, (x - jnp.arange(4)) % 4, axis=0).reshape(half.shape)
    return join_core(half, core)


def sum_all_swap(gram):
    axes = ("author", "word")
    devices = lax.axis_size(axes)
    parts = lax.all_to_all(gram.reshape(devices, -1, gram.shape[1]), axes, 0, 0)
    rows = jnp.sum(parts, axis=0)
    rows = jnp.broadcast_to(rows[None], (devices,) + rows.shape)
    return lax.all_to_all(rows, axes, 0, 0).reshape(gram.shape)


def eliminate(strips):
    shape = strips[0].shape
    sub = lax.broadcasted_iota(jnp.int32, shape, 0)
    half = shape[1] // 2

    def column(strip, lane):
        return jnp.broadcast_to(strip[:, lane : lane + 1], shape)

    def row(strip, j):
        return jnp.broadcast_to(strip[j : j + 1, :], shape)

    for p in range(len(strips)):
        lead = strips[p]
        lanes = [half + 8 * p + j for j in range(8)]
        cols = [column(lead, lane) for lane in lanes]
        below = {i: [column(strips[i], lane) for lane in lanes] for i in range(p + 1, len(strips))}
        scale = jnp.zeros(shape, jnp.float32)
        for j in range(0, 8, 2):
            a, b, c = row(cols[j], j), row(cols[j + 1], j), row(cols[j + 1], j + 1)
            inv0 = 1.0 / a
            inv1 = a / (a * c - b * b)
            m0 = jnp.where(sub > j, cols[j] * inv0, 0.0)
            m1 = jnp.where(sub > j + 1, (cols[j + 1] - m0 * b) * inv1, 0.0)
            top0 = row(lead, j)
            top1 = row(lead, j + 1) - (b * inv0) * top0
            lead = (lead - m0 * top0) - m1 * top1
            scale = jnp.where(sub == j, lax.rsqrt(a), scale)
            scale = jnp.where(sub == j + 1, jnp.sqrt(inv1), scale)
            tops = []
            for k in range(j + 2, 8):
                u0 = row(cols[k], j)
                u1 = row(cols[k], j + 1) - (b * inv0) * u0
                cols[k] = (cols[k] - m0 * u0) - m1 * u1
                tops.append((u0, u1))
            for i, col in below.items():
                n0 = col[j] * inv0
                n1 = (col[j + 1] - n0 * b) * inv1
                for k, (u0, u1) in zip(range(j + 2, 8), tops):
                    col[k] = (col[k] - n0 * u0) - n1 * u1
                strips[i] = (strips[i] - n0 * top0) - n1 * top1
        strips[p] = lead * scale
    return strips


def whiten_kernel(g_ref, out_ref, s_ref, y_ref):
    n = g_ref.shape[0]
    g = g_ref[...]
    eye = lax.broadcasted_iota(jnp.int32, (n, n), 0) == lax.broadcasted_iota(jnp.int32, (n, n), 1)
    diag = jnp.where(eye, g, 0.0)
    across = lax.rsqrt(jnp.sum(diag, axis=0, keepdims=True))
    down = lax.rsqrt(jnp.sum(diag, axis=1, keepdims=True))
    s_ref[...] = g * across * down
    y_ref[...] = jnp.where(eye, 1.0, 0.0)
    lane = lax.broadcasted_iota(jnp.int32, (BLOCK, n), 1)
    def stage(at, carry):
        rows = pl.ds(pl.multiple_of(at * BLOCK, BLOCK), BLOCK)
        left, right = s_ref[rows, :], y_ref[rows, :]
        turned = pltpu.roll(left, lax.rem(n + BLOCK - at * BLOCK, n), 1)[:, : 2 * BLOCK]
        i0 = lax.broadcasted_iota(jnp.int32, turned.shape, 0)
        i1 = lax.broadcasted_iota(jnp.int32, turned.shape, 1)
        start = jnp.where(i1 < BLOCK, jnp.where(i0 == i1, 1.0, 0.0), turned)
        strips = eliminate([start[8 * i : 8 * i + 8] for i in range(BLOCK // 8)])
        inverse = jnp.concatenate(strips, axis=0)[:, :BLOCK]
        dot = lambda u, v, d: lax.dot_general(u, v, (((d,), (0,)), ((), ())), precision=HIGH, preferred_element_type=jnp.float32)
        left = dot(inverse, left, 1)
        right = dot(inverse, right, 1)

        @pl.when(at + 1 < n // BLOCK)
        def _():
            rest = jnp.where(lane >= (at + 1) * BLOCK, left, 0.0)
            s_ref[...] -= dot(rest, left, 0)
            y_ref[...] -= dot(rest, right, 0)

        y_ref[rows, :] = right
        return carry
    lax.fori_loop(0, n // BLOCK, stage, 0)
    out_ref[...] = y_ref[...] * across


def whitener(gram):
    return pl.pallas_call(
        whiten_kernel,
        out_shape=jax.ShapeDtypeStruct(gram.shape, jnp.float32),
        scratch_shapes=[pltpu.VMEM(gram.shape, jnp.float32)] * 2,
        cost_estimate=pl.CostEstimate(flops=10**9, bytes_accessed=40 * 10**6, transcendentals=0),
        name="whitener",
    )(gram)


def apply_t(field, inverse, precision=MIDDLE):
    return lax.dot_general(
        field, inverse, (((1,), (1,)), ((), ())), precision=precision, preferred_element_type=jnp.float32
    )


def short(array):
    return array.astype(jnp.bfloat16)


def long(array):
    return array.astype(jnp.float32)


def ring_places():
    core = lax.axis_index("author") % 2
    y, z = lax.axis_index("word") // 4, lax.axis_index("word") % 4
    return core, jnp.where(core == 0, z, y), jnp.where(core == 0, y, z)


def hop_ring(array, ring, k):
    pairs = []
    for device in range(128):
        core, y, z = device // 16 % 2, device % 16 // 4, device % 4
        if core == ring:
            z = (z + k) % 4
        else:
            y = (y + k) % 4
        pairs.append((device, device // 16 * 16 + y * 4 + z))
    return lax.ppermute(array, ("author", "word"), pairs)


def scatter_word(terms):
    _, one, two = ring_places()
    terms = terms.reshape(4, 4, -1, terms.shape[1])
    got = [hop_ring(pick(terms, (one + k) % 4), 0, k) for k in (2, 1, 3)]
    terms = short(long(pick(terms, one)) + long(got[0]) + long(got[1]) + long(got[2]))
    got = [hop_ring(pick(terms, (two + k) % 4), 1, k) for k in (2, 1, 3)]
    return [pick(terms, two)] + got


def gather_word(share):
    line = jnp.stack([share] + [hop_ring(share, 1, k) for k in (1, 2, 3)])
    return jnp.concatenate([line] + [hop_ring(line, 0, k) for k in (1, 2, 3)])


def ring_rows(rows):
    core, one, two = ring_places()
    share = rows // 2
    y, z = share // 4, share % 4
    first, second = jnp.where(core == 0, z, y), jnp.where(core == 0, y, z)
    return ((one - first) % 4 * 4 + (two - second) % 4) * 2 + rows % 2


def shards(block_values, block_rows, block_cols, block_count, omega):
    values = block_values[0, 0]
    rows = block_rows[0, 0]
    cols = block_cols[0, 0]
    count = block_count[0, 0]
    size = values.shape[1]
    word_blocks = omega.shape[0] // size
    author_blocks = 32
    authors = author_blocks * size * lax.axis_size("author")
    words = word_blocks * size * lax.axis_size("word")
    wide = omega
    word_factor = None
    for turn in range(ITERS):
        terms = product(values, cols, rows, count, ring_places()[0], wide, author_blocks)
        y, brief = fold(scatter_word(terms), word_factor)
        y_rows = gather_word(brief).reshape(terms.shape)
        terms = product_t(values, ring_rows(rows), cols, count, y_rows, word_blocks)
        z = long(lax.psum_scatter(terms, "author", scatter_dimension=0, tiled=True))
        author_factor = whitener(sum_author(gram_short(y_rows)) / authors)
        z = apply_t(z, author_factor)
        gram = (sum_all if turn + 1 < ITERS else sum_all_swap)(gram_of(z)) / words
        if turn + 1 < ITERS:
            wide = lax.all_gather(short(z), "author", axis=0, tiled=True)
            wide, word_factor = lax.optimization_barrier((wide, whitener(gram)))
        else:
            word_factor = whitener(gram)
    author_basis = short(apply_t(y, author_factor))
    word_basis = short(apply_t(z, word_factor))
    return (author_basis, word_basis)


def solution(mesh):
    return jax.shard_map(
        shards,
        mesh=mesh,
        in_specs=(
            P("author", "word", None, None, None),
            P("author", "word", None),
            P("author", "word", None),
            P("author", "word"),
            P("word", None),
        ),
        out_specs=(P(("author", "word"), None), P(("word", "author"), None)),
        check_vma=False,
    )
```

```python
import jax
import jax.numpy as jnp
from jax import lax
from jax.experimental import pallas as pl
from jax.experimental.pallas import tpu as pltpu
from jax.sharding import PartitionSpec as P

ITERS = 2
GROUP = 16
CUT = 2048
BLOCK = 64
HIGH = lax.Precision.HIGHEST
MIDDLE = lax.Precision.HIGH


def product_kernel(
    src_ids, dst_ids, count, core, values, given, out, total, part, panel, part_sem, panel_sem
):
    size = part.shape[1]
    groups = (count[0] + GROUP - 1) // GROUP

    def fetch(group):
        span = pl.ds(group * GROUP, GROUP)
        return pltpu.make_async_copy(values.at[span], part.at[span], part_sem.at[group])

    def start(group, carry):
        fetch(group).start()
        return carry

    def clear(index, carry):
        total[index] = jnp.zeros_like(total[index])
        return carry

    def work(group, carry):
        fetch(group).wait()
        first = group * GROUP
        prods = []
        for offset in range(GROUP):
            rows = pl.ds(pl.multiple_of(src_ids[first + offset] * size, size), size)
            prods.append(jnp.dot(part[first + offset], panel[rows, :], preferred_element_type=jnp.float32))
        for offset in range(GROUP):
            total[dst_ids[first + offset]] += prods[offset]
        return carry

    def emit(index, carry):
        share, row = index // 2, index % 2
        place = jnp.where(core[0] == 0, share % 4 * 4 + share // 4, share) * 2 + row
        out[pl.ds(pl.multiple_of(place * size, size), size), :] = total[index].astype(out.dtype)
        return carry

    moves = []
    for index in range(panel_sem.shape[0]):
        rows = pl.ds(index * CUT, CUT)
        moves.append(pltpu.make_async_copy(given.at[rows], panel.at[rows], panel_sem.at[index]))
    fetch(0).start()
    for move in moves:
        move.start()
    lax.fori_loop(1, groups, start, 0)
    lax.fori_loop(0, total.shape[0], clear, 0)
    for move in moves:
        move.wait()
    lax.fori_loop(0, groups, work, 0)
    lax.fori_loop(0, out.shape[0] // size, emit, 0)


def product_t_kernel(src_ids, dst_ids, count, values, *refs):
    pieces, (out, total, part, staged, panel, part_sem, out_sem, piece_sem) = refs[:-8], refs[-8:]
    size = part.shape[1]
    moves = []
    for index, piece in enumerate(pieces):
        target = panel.at[pl.ds(index * piece.shape[0], piece.shape[0])]
        moves.append(pltpu.make_async_copy(piece, target, piece_sem.at[index]))
        moves[-1].start()
    groups = (count[0] + GROUP - 1) // GROUP

    def fetch(group):
        span = pl.ds(group * GROUP, GROUP)
        return pltpu.make_async_copy(values.at[span], part.at[span], part_sem.at[group])

    def start(group, carry):
        fetch(group).start()
        return carry

    def clear(index, carry):
        total[index] = jnp.zeros_like(total[index])
        return carry

    def work(group, carry):
        fetch(group).wait()
        first = group * GROUP
        prods = []
        for offset in range(GROUP):
            rows = pl.ds(pl.multiple_of(src_ids[first + offset] * size, size), size)
            prods.append(
                lax.dot_general(
                    part[first + offset],
                    panel[rows, :],
                    (((0,), (0,)), ((), ())),
                    preferred_element_type=jnp.float32,
                )
            )
        for offset in range(GROUP):
            total[dst_ids[first + offset]] += prods[offset]
        return carry

    def emit(index, carry):
        staged[pl.ds(pl.multiple_of(index * size, size), size), :] = total[index].astype(staged.dtype)
        return carry

    lax.fori_loop(0, groups, start, 0)
    lax.fori_loop(0, total.shape[0], clear, 0)
    for move in moves:
        move.wait()
    lax.fori_loop(0, groups, work, 0)
    blocks = out.shape[0] // size
    pieces = out_sem.shape[0]
    sends = []
    for piece in range(pieces):
        lax.fori_loop(piece * blocks // pieces, (piece + 1) * blocks // pieces, emit, 0)
        rows = pl.ds(piece * out.shape[0] // pieces, out.shape[0] // pieces)
        sends.append(pltpu.make_async_copy(staged.at[rows], out.at[rows], out_sem.at[piece]))
        sends[-1].start()
    for send in sends:
        send.wait()


def kernel_call(kernel, name, operands, specs, out, cap, size, scratch):
    rows, width = out.shape
    return pl.pallas_call(
        kernel,
        out_shape=out,
        in_specs=specs,
        out_specs=pl.BlockSpec(memory_space=pltpu.VMEM if name == "product" else pl.ANY),
        scratch_shapes=[
            pltpu.VMEM((rows // size + 1, size, width), jnp.float32),
            pltpu.VMEM((cap, size, size), jnp.bfloat16),
            *scratch,
        ],
        compiler_params=pltpu.CompilerParams(vmem_limit_bytes=36 * 1024 * 1024),
        cost_estimate=pl.CostEstimate(
            flops=4 * cap * size * size * width, bytes_accessed=20 * 1024 * 1024, transcendentals=0
        ),
        name=name,
    )(*operands)


def product(values, cols, rows, count, core, panel, out_blocks):
    cap, size, _ = values.shape
    width = panel.shape[1]
    rows = jnp.where(jnp.arange(cap, dtype=jnp.int32) < count, rows, out_blocks)
    smem = pl.BlockSpec(memory_space=pltpu.SMEM)
    whole = pl.BlockSpec(memory_space=pl.ANY)
    values = pltpu.with_memory_space_constraint(values, pltpu.HBM)
    panel = pltpu.with_memory_space_constraint(panel, pltpu.HBM)
    scratch = [
        pltpu.VMEM(panel.shape, jnp.bfloat16),
        pltpu.SemaphoreType.DMA((cap // GROUP,)),
        pltpu.SemaphoreType.DMA((panel.shape[0] // CUT,)),
    ]
    operands = (cols, rows, count.reshape(1), core.reshape(1), values, panel)
    specs = [smem] * 4 + [whole] * 2
    out = pltpu.VMEM((out_blocks * size, width), jnp.bfloat16)
    return kernel_call(product_kernel, "product", operands, specs, out, cap, size, scratch)


def product_t(values, rows, cols, count, pieces, out_blocks):
    cap, size, _ = values.shape
    cols = jnp.where(jnp.arange(cap, dtype=jnp.int32) < count, cols, out_blocks)
    smem = pl.BlockSpec(memory_space=pltpu.SMEM)
    whole = pl.BlockSpec(memory_space=pl.ANY)
    width = pieces[0].shape[1]
    values = pltpu.with_memory_space_constraint(values, pltpu.HBM)
    out = pltpu.HBM((out_blocks * size, width), jnp.bfloat16)
    scratch = [
        pltpu.VMEM(out.shape, jnp.bfloat16),
        pltpu.VMEM((sum(piece.shape[0] for piece in pieces), width), jnp.bfloat16),
        pltpu.SemaphoreType.DMA((cap // GROUP,)),
        pltpu.SemaphoreType.DMA((8,)),
        pltpu.SemaphoreType.DMA((len(pieces),)),
    ]
    operands = (rows, cols, count.reshape(1), values, *pieces)
    specs = [smem] * 3 + [whole] * (1 + len(pieces))
    return kernel_call(product_t_kernel, "product_t", operands, specs, out, cap, size, scratch)


def fold_kernel(parts, factor, field, brief):
    total = parts[0][...].astype(jnp.float32)
    for part in parts[1:]:
        total += part[...].astype(jnp.float32)
    if factor is not None:
        total = apply_t(total, factor[...], HIGH)
    field[...] = total
    brief[...] = total.astype(brief.dtype)


def fold(parts, factor):
    vmem = pl.BlockSpec(memory_space=pltpu.VMEM)
    count = len(parts)
    operands = list(parts) + ([] if factor is None else [factor])

    def kernel(*refs):
        fold_kernel(refs[:count], refs[count] if factor is not None else None, *refs[-2:])

    return pl.pallas_call(
        kernel,
        out_shape=(
            jax.ShapeDtypeStruct(parts[0].shape, jnp.float32),
            jax.ShapeDtypeStruct(parts[0].shape, jnp.bfloat16),
        ),
        in_specs=[vmem] * len(operands),
        out_specs=(vmem, vmem),
        name="fold",
    )(*operands)


def gram_kernel(*refs):
    out = refs[-1]
    total = jnp.zeros(out.shape, jnp.float32)
    step = 512
    for piece in refs[:-1]:
        for start in range(0, piece.shape[0], step):
            part = piece[pl.ds(start, step), :]
            total += lax.dot_general(part, part, (((0,), (0,)), ((), ())), preferred_element_type=jnp.float32)
    out[...] = total


def gram_short(pieces):
    vmem = pl.BlockSpec(memory_space=pltpu.VMEM)
    return pl.pallas_call(
        gram_kernel,
        out_shape=jax.ShapeDtypeStruct((pieces[0].shape[1],) * 2, jnp.float32),
        in_specs=[vmem] * len(pieces),
        out_specs=vmem,
        name="gram_short",
    )(*pieces)


def gram_of(field):
    return lax.dot_general(
        field, field, (((0,), (0,)), ((), ())), precision=MIDDLE, preferred_element_type=jnp.float32
    )


def hop_core(array):
    return lax.ppermute(array, "author", [(i, i ^ 1) for i in range(8)])


def hop_x(array, k):
    return lax.ppermute(array, "author", [(i, (i + 2 * k) % 8) for i in range(8)])


def hop_y(array, k):
    return lax.ppermute(array, "word", [(i, (i + 4 * k) % 16) for i in range(16)])


def hop_z(array, k):
    return lax.ppermute(array, "word", [(i, (i // 4) * 4 + (i + k) % 4) for i in range(16)])


def pick(array, index):
    return lax.dynamic_index_in_dim(array, index, 0, keepdims=False)


def split_core(gram, core):
    halves = gram.reshape(2, gram.shape[0] // 2, gram.shape[1])
    return pick(halves, core) + hop_core(pick(halves, 1 - core))


def join_core(half, core):
    other = hop_core(half)
    return jnp.where(core == 0, jnp.concatenate([half, other]), jnp.concatenate([other, half]))


def sum_author(gram):
    core = lax.axis_index("author") % 2
    half = split_core(gram, core)
    parts = [hop_x(half, k) for k in (1, 3, 2)]
    half = (half + parts[2]) + (parts[0] + parts[1])
    return join_core(half, core)


def sum_all(gram):
    place = lax.axis_index("author")
    core, x = place % 2, place // 2
    half = split_core(gram, core)
    chunks = half.reshape(4, half.shape[0] // 4, half.shape[1])
    got = [hop_x(pick(chunks, (x + k) % 4), k) for k in (1, 3, 2)]
    part = (pick(chunks, x) + got[2]) + (got[0] + got[1])
    for hop in (hop_y, hop_z):
        got = [hop(part, k) for k in (1, 3, 2)]
        part = (part + got[2]) + (got[0] + got[1])
    ring = jnp.stack([part] + [hop_x(part, k) for k in (1, 2, 3)])
    half = jnp.take(ring, (x - jnp.arange(4)) % 4, axis=0).reshape(half.shape)
    return join_core(half, core)


def sum_all_swap(gram):
    axes = ("author", "word")
    devices = lax.axis_size(axes)
    parts = lax.all_to_all(gram.reshape(devices, -1, gram.shape[1]), axes, 0, 0)
    rows = jnp.sum(parts, axis=0)
    rows = jnp.broadcast_to(rows[None], (devices,) + rows.shape)
    return lax.all_to_all(rows, axes, 0, 0).reshape(gram.shape)


def eliminate(strips):
    shape = strips[0].shape
    sub = lax.broadcasted_iota(jnp.int32, shape, 0)
    half = shape[1] // 2

    def column(strip, lane):
        return jnp.broadcast_to(strip[:, lane : lane + 1], shape)

    def row(strip, j):
        return jnp.broadcast_to(strip[j : j + 1, :], shape)

    for p in range(len(strips)):
        lead = strips[p]
        lanes = [half + 8 * p + j for j in range(8)]
        cols = [column(lead, lane) for lane in lanes]
        below = {i: [column(strips[i], lane) for lane in lanes] for i in range(p + 1, len(strips))}
        scale = jnp.zeros(shape, jnp.float32)
        for j in range(0, 8, 2):
            a, b, c = row(cols[j], j), row(cols[j + 1], j), row(cols[j + 1], j + 1)
            inv0 = 1.0 / a
            inv1 = a / (a * c - b * b)
            m0 = jnp.where(sub > j, cols[j] * inv0, 0.0)
            m1 = jnp.where(sub > j + 1, (cols[j + 1] - m0 * b) * inv1, 0.0)
            top0 = row(lead, j)
            top1 = row(lead, j + 1) - (b * inv0) * top0
            lead = (lead - m0 * top0) - m1 * top1
            scale = jnp.where(sub == j, lax.rsqrt(a), scale)
            scale = jnp.where(sub == j + 1, jnp.sqrt(inv1), scale)
            tops = []
            for k in range(j + 2, 8):
                u0 = row(cols[k], j)
                u1 = row(cols[k], j + 1) - (b * inv0) * u0
                cols[k] = (cols[k] - m0 * u0) - m1 * u1
                tops.append((u0, u1))
            for i, col in below.items():
                n0 = col[j] * inv0
                n1 = (col[j + 1] - n0 * b) * inv1
                for k, (u0, u1) in zip(range(j + 2, 8), tops):
                    col[k] = (col[k] - n0 * u0) - n1 * u1
                strips[i] = (strips[i] - n0 * top0) - n1 * top1
        strips[p] = lead * scale
    return strips


def whiten_kernel(g_ref, out_ref, s_ref, y_ref):
    n = g_ref.shape[0]
    g = g_ref[...]
    eye = lax.broadcasted_iota(jnp.int32, (n, n), 0) == lax.broadcasted_iota(jnp.int32, (n, n), 1)
    diag = jnp.where(eye, g, 0.0)
    across = lax.rsqrt(jnp.sum(diag, axis=0, keepdims=True))
    down = lax.rsqrt(jnp.sum(diag, axis=1, keepdims=True))
    s_ref[...] = g * across * down
    y_ref[...] = jnp.where(eye, 1.0, 0.0)
    lane = lax.broadcasted_iota(jnp.int32, (BLOCK, n), 1)
    def stage(at, carry):
        rows = pl.ds(pl.multiple_of(at * BLOCK, BLOCK), BLOCK)
        left, right = s_ref[rows, :], y_ref[rows, :]
        turned = pltpu.roll(left, lax.rem(n + BLOCK - at * BLOCK, n), 1)[:, : 2 * BLOCK]
        i0 = lax.broadcasted_iota(jnp.int32, turned.shape, 0)
        i1 = lax.broadcasted_iota(jnp.int32, turned.shape, 1)
        start = jnp.where(i1 < BLOCK, jnp.where(i0 == i1, 1.0, 0.0), turned)
        strips = eliminate([start[8 * i : 8 * i + 8] for i in range(BLOCK // 8)])
        inverse = jnp.concatenate(strips, axis=0)[:, :BLOCK]
        dot = lambda u, v, d: lax.dot_general(u, v, (((d,), (0,)), ((), ())), precision=HIGH, preferred_element_type=jnp.float32)
        left = dot(inverse, left, 1)
        right = dot(inverse, right, 1)

        @pl.when(at + 1 < n // BLOCK)
        def _():
            rest = jnp.where(lane >= (at + 1) * BLOCK, left, 0.0)
            s_ref[...] -= dot(rest, left, 0)
            y_ref[...] -= dot(rest, right, 0)

        y_ref[rows, :] = right
        return carry
    lax.fori_loop(0, n // BLOCK, stage, 0)
    out_ref[...] = y_ref[...] * across


def whitener(gram):
    return pl.pallas_call(
        whiten_kernel,
        out_shape=jax.ShapeDtypeStruct(gram.shape, jnp.float32),
        scratch_shapes=[pltpu.VMEM(gram.shape, jnp.float32)] * 2,
        cost_estimate=pl.CostEstimate(flops=10**9, bytes_accessed=40 * 10**6, transcendentals=0),
        name="whitener",
    )(gram)


def apply_t(field, inverse, precision=MIDDLE):
    return lax.dot_general(
        field, inverse, (((1,), (1,)), ((), ())), precision=precision, preferred_element_type=jnp.float32
    )


def short(array):
    return array.astype(jnp.bfloat16)


def long(array):
    return array.astype(jnp.float32)


def ring_places():
    core = lax.axis_index("author") % 2
    y, z = lax.axis_index("word") // 4, lax.axis_index("word") % 4
    return core, jnp.where(core == 0, z, y), jnp.where(core == 0, y, z)


def hop_ring(array, ring, k):
    pairs = []
    for device in range(128):
        core, y, z = device // 16 % 2, device % 16 // 4, device % 4
        if core == ring:
            z = (z + k) % 4
        else:
            y = (y + k) % 4
        pairs.append((device, device // 16 * 16 + y * 4 + z))
    return lax.ppermute(array, ("author", "word"), pairs)


def scatter_word(terms):
    _, one, two = ring_places()
    terms = terms.reshape(4, 4, -1, terms.shape[1])
    got = [hop_ring(pick(terms, (one + k) % 4), 0, k) for k in (2, 1, 3)]
    terms = short(long(pick(terms, one)) + long(got[0]) + long(got[1]) + long(got[2]))
    got = [hop_ring(pick(terms, (two + k) % 4), 1, k) for k in (2, 1, 3)]
    return [pick(terms, two)] + got


def gather_word(share):
    line = jnp.stack([share] + [hop_ring(share, 1, k) for k in (1, 2, 3)])
    lines = [line] + [hop_ring(line, 0, k) for k in (1, 2, 3)]
    return [line.reshape(-1, share.shape[1]) for line in lines]


def ring_rows(rows):
    core, one, two = ring_places()
    share = rows // 2
    y, z = share // 4, share % 4
    first, second = jnp.where(core == 0, z, y), jnp.where(core == 0, y, z)
    return ((one - first) % 4 * 4 + (two - second) % 4) * 2 + rows % 2


def shards(block_values, block_rows, block_cols, block_count, omega):
    values = block_values[0, 0]
    rows = block_rows[0, 0]
    cols = block_cols[0, 0]
    count = block_count[0, 0]
    size = values.shape[1]
    word_blocks = omega.shape[0] // size
    author_blocks = 32
    authors = author_blocks * size * lax.axis_size("author")
    words = word_blocks * size * lax.axis_size("word")
    wide = omega
    word_factor = None
    for turn in range(ITERS):
        terms = product(values, cols, rows, count, ring_places()[0], wide, author_blocks)
        y, brief = fold(scatter_word(terms), word_factor)
        y_rows = gather_word(brief)
        terms = product_t(values, ring_rows(rows), cols, count, y_rows, word_blocks)
        z = long(lax.psum_scatter(terms, "author", scatter_dimension=0, tiled=True))
        author_factor = whitener(sum_author(gram_short(y_rows)) / authors)
        z = apply_t(z, author_factor)
        gram = (sum_all if turn + 1 < ITERS else sum_all_swap)(gram_of(z)) / words
        if turn + 1 < ITERS:
            wide = lax.all_gather(short(z), "author", axis=0, tiled=True)
            wide, word_factor = lax.optimization_barrier((wide, whitener(gram)))
        else:
            word_factor = whitener(gram)
    author_basis = short(apply_t(y, author_factor))
    word_basis = short(apply_t(z, word_factor))
    return (author_basis, word_basis)


def solution(mesh):
    return jax.shard_map(
        shards,
        mesh=mesh,
        in_specs=(
            P("author", "word", None, None, None),
            P("author", "word", None),
            P("author", "word", None),
            P("author", "word"),
            P("word", None),
        ),
        out_specs=(P(("author", "word"), None), P(("word", "author"), None)),
        check_vma=False,
    )
```
